32 devices in a mesh: fsdp: 8 (over z, x), tp: 4 (over y, core).
Axes of the slice: x: 2, y: 2, z: 4, core: 2. Of those that a mesh axis runs over, the one named last changes fastest.
Arguments:
- tokens: bfloat16 [16384, 768], P(('fsdp', 'tp')), may hold values from -6 to 6
- seq_lengths: int32 [8, 8], P('fsdp'), may hold values from 1 to 1024, 2048 in all within a row
- w_qkv: bfloat16 [3, 768, 768], P(None, 'fsdp', 'tp'), may hold values from -0.21875 to 0.21875
- w_out: bfloat16 [768, 768], P('tp', 'fsdp'), may hold values from -1.25 to 1.25
- w_in: bfloat16 [2, 768, 1152], P(None, 'fsdp', 'tp'), may hold values from -0.21875 to 0.21875
- w_down: bfloat16 [1152, 768], P('tp', 'fsdp'), may hold values from -0.1875 to 0.1875
- gains: bfloat16 [2, 768], P(None, 'fsdp'), may hold values from 0.5 to 1.5
- cotangent: bfloat16 [16384, 768], P(('fsdp', 'tp')), may hold values from -6 to 6
Outputs:
- output: bfloat16 [16384, 768], P(('fsdp', 'tp'))
- grad_tokens: bfloat16 [16384, 768], P(('fsdp', 'tp'))
- grad_qkv: float32 [3, 768, 768], P(None, 'fsdp', 'tp')
- grad_out: float32 [768, 768], P('tp', 'fsdp')
- grad_in: float32 [2, 768, 1152], P(None, 'fsdp', 'tp')
- grad_down: float32 [1152, 768], P('tp', 'fsdp')
- grad_gains: float32 [2, 768], P(None, 'fsdp')
The draws below stay inside these ranges and needn't reach their ends.
Inputs may be any that keep to these rules, and one draw needn't show every extreme that they name: `seq_lengths`: each row of a group holds 8 lengths that add up to 2048; the longest of each group is exactly 1024.
All inputs are finite; a program needn't handle non-finite values.
Results may differ from the reference program's by a relative error of at most 0.018.
Values may be sent and summed in bfloat16 or wider, within the bound.
No kernel may reach another device: no remote copies, remote signals or barrier semaphores. Data moves between devices by JAX's collectives and lax.ppermute only.
A program may use at most 128 MiB of HBM per device.

```python
import math
import jax
import jax.numpy as jnp
import numpy as np
from jax import lax

D = 768
HEADS = 12
HEAD_DIM = 64
FF = 1152
SEQS = 8
GROUP = 2048
TOKENS = 16384
LONGEST = 1024
N_FSDP = 8


def with_spikes(array, own_key, source, target, parts, factor):
    owner, partner = [(jnp.arange(array.shape[axis_at]) // (array.shape[axis_at] // parts)).reshape([-1 if axis == axis_at else 1 for axis in range(array.ndim)]) for axis_at in (source, target)]
    chosen = jax.random.permutation(own_key, parts)[partner]
    strong = (owner == chosen) | (owner == (partner + parts // 2) % parts)
    return jnp.where(strong, factor * array, array)


def block_scale(key, extent, cuts, least, high):
    level, own = 1.0, jax.random.fold_in(key, 6)
    for position, shards_of in cuts:
        steps = jnp.exp(jax.random.uniform(jax.random.fold_in(own, position), (shards_of,), jnp.float32, least / len(cuts), high / len(cuts)))
        level = level * jnp.repeat(steps, extent[position] // shards_of).reshape([-1 if axis == position else 1 for axis in range(len(extent))])
    return level


def length_profile(amount, total, most, slope):
    loads = [(1 << 20) // math.isqrt(grade ** slope) + 1 for grade in range(2, amount + 1)]
    spare, given = total - most - (amount - 1), [1] * (amount - 1)
    while spare > 0:
        free = [i for i in range(amount - 1) if given[i] < most]
        whole, remaining = sum([loads[i] for i in free]), spare
        for i in free:
            extra = min(most - given[i], max(1, remaining * loads[i] // whole), spare)
            given[i] = given[i] + extra
            spare = spare - extra
    return np.array([most] + given)


def ragged(rng, count, total, reach, skew):
    if count == 2:
        one = jax.random.randint(rng, (), max(1, total - reach), min(reach, total - 1) + 1)
        return jnp.stack([one, total - one])
    tallies = jnp.asarray(length_profile(count, total, reach, skew), jnp.int32)
    twos = (count - 1) // 2
    source_of, taker = tallies[1:1 + 2 * twos:2], tallies[2:2 + 2 * twos:2]
    slack = jnp.minimum(source_of - 1, reach - taker)
    moved = jax.random.randint(jax.random.fold_in(rng, 1), (twos,), 0, 1 << 20) % (slack + 1)
    tallies = tallies.at[1:1 + 2 * twos:2].set(source_of - moved).at[2:2 + 2 * twos:2].set(taker + moved)
    return tallies[jax.random.permutation(jax.random.fold_in(rng, 2), count)]


def bell_draw(stream_key, extent, width, reach, pieces=(), kind=jnp.bfloat16):
    level = block_scale(stream_key, extent, pieces, -0.22, 0.18) if pieces else 1.0
    values = jax.random.normal(stream_key, extent, jnp.float32) * width * level
    return jnp.minimum(jnp.maximum(values, -reach), reach).astype(kind)


def gaussian_with(stream_key, shape, deviation, limit, pieces, heavy, kind=jnp.bfloat16):
    entries = deviation * jax.random.normal(stream_key, shape, jnp.float32)
    if pieces:
        entries = entries * block_scale(stream_key, shape, pieces, -0.22, 0.18)
    return jnp.clip(with_spikes(entries, jax.random.fold_in(stream_key, 3), *heavy), -limit, limit).astype(kind)


def setup_inputs(seed: int = 0) -> dict:
    splits = jax.random.split(jax.random.key(seed), 9)
    return {
        "tokens": bell_draw(splits[0], (TOKENS, D), 1.0, 6.0, ((0, 32),)),
        "seq_lengths": jax.vmap(lambda own: ragged(own, SEQS, GROUP, LONGEST, 2))(jax.random.split(splits[1], N_FSDP)).reshape((N_FSDP, SEQS)).astype(jnp.int32),
        "w_qkv": bell_draw(splits[2], (3, D, D), D ** -0.5, 0.21875, ((1, 8), (2, 4))),
        "w_out": bell_draw(splits[3], (D, D), (max(D // 32, 1)) ** -0.5, 1.25, ((0, 4), (1, 8))),
        "w_in": bell_draw(splits[4], (2, D, FF), D ** -0.5, 0.21875, ((1, 8), (2, 4))),
        "w_down": bell_draw(splits[5], (FF, D), FF ** -0.5, 0.1875, ((0, 4), (1, 8))),
        "gains": jnp.clip(1.0 + 0.1 * jax.random.normal(splits[6], (2, D), jnp.float32), 0.5, 1.5).astype(jnp.bfloat16),
        "cotangent": gaussian_with(splits[7], (TOKENS, D), 1.0, 6.0, ((0, 32),), (0, 1, 32, 2.75)),
    }


@jax.custom_vjp
def low(v):
    return lax.optimization_barrier(v.astype(jnp.bfloat16)).astype(jnp.float32)

@jax.custom_vjp
def low_back(v):
    return v

def low_keep(v):
    return (low(v), None)

def low_pass(kept, grad):
    return (grad,)

def back_keep(v):
    return (v, None)

def back_low(kept, grad):
    return (low(grad),)
low.defvjp(low_keep, low_pass)
low_back.defvjp(back_keep, back_low)

def matmul(left, right):
    return jnp.dot(left, right, precision=lax.Precision.HIGHEST)

def norm_rows(values, gain):
    center = values - lax.optimization_barrier(jnp.mean(values, axis=-1, keepdims=True))
    spread = lax.optimization_barrier(jnp.mean(center * center, axis=-1, keepdims=True))
    return center * lax.rsqrt(spread + 1e-05) * gain

def positions(lengths, total):
    lengths = lengths.astype(jnp.int32)
    ends = jnp.cumsum(lengths).astype(jnp.int32)
    starts = (ends - lengths).astype(jnp.int32)
    index = jnp.arange(total, dtype=jnp.int32)
    segment = lax.optimization_barrier(jnp.sum((index[:, None] >= ends[None, :]).astype(jnp.int32), axis=1)).astype(jnp.int32)
    onehot = segment[:, None] == jnp.arange(lengths.shape[0], dtype=jnp.int32)[None, :]
    first = lax.optimization_barrier(jnp.sum(jnp.where(onehot, starts[None, :], 0), axis=1)).astype(jnp.int32)
    return (segment, (index - first).astype(jnp.int32))

def rope_tables(place, size):
    half = size // 2
    freq = jnp.exp(-jnp.log(jnp.float32(160000.0)) * jnp.arange(half, dtype=jnp.float32) * (2.0 / size))
    angle = place.astype(jnp.float32)[:, None] * freq[None, :]
    return (jnp.cos(angle), jnp.sin(angle))

def rotate(values, cosine, sine):
    half = values.shape[-1] // 2
    first = values[..., :half]
    second = values[..., half:]
    cos_b = cosine[:, None, :]
    sin_b = sine[:, None, :]
    return jnp.concatenate([first * cos_b - second * sin_b, second * cos_b + first * sin_b], axis=-1)

def group_layer(params, rows_in, lengths):
    w_qkv, w_out, w_in, w_down, gains = params
    group = rows_in.shape[0]
    segment, place = positions(lengths, group)
    cosine, sine = rope_tables(place, HEAD_DIM)
    normed1 = low(norm_rows(rows_in, gains[0]))
    q_raw = low_back(matmul(normed1, w_qkv[0])).reshape(group, HEADS, HEAD_DIM)
    k_raw = low_back(matmul(normed1, w_qkv[1])).reshape(group, HEADS, HEAD_DIM)
    values = low(low_back(matmul(normed1, w_qkv[2]))).reshape(group, HEADS, HEAD_DIM)
    query = low(rotate(q_raw, cosine, sine))
    keys = low(rotate(k_raw, cosine, sine))
    block = min(512, group)
    count = group // block
    scale = HEAD_DIM ** (-0.5)

    def attend(pair):
        q_block, seg_block = pair
        raw = low_back(jnp.einsum('qhd,khd->hqk', q_block, keys, precision=lax.Precision.HIGHEST))
        same = (seg_block[:, None] == segment[None, :])[None]
        scores = jnp.where(same, raw * scale, -1e+30)
        top = lax.optimization_barrier(jnp.max(scores, axis=-1, keepdims=True))
        expo = jnp.exp(scores - top)
        probs = low(expo / lax.optimization_barrier(jnp.sum(expo, axis=-1, keepdims=True)))
        return jnp.einsum('hqk,khd->qhd', probs, values, precision=lax.Precision.HIGHEST)
    ctx = lax.map(jax.checkpoint(attend), (query.reshape(count, block, HEADS, HEAD_DIM), segment.reshape(count, block)))
    context = low(low_back(ctx.reshape(group, D)))
    h_mid = rows_in + low_back(matmul(context, w_out))
    normed2 = low(norm_rows(h_mid, gains[1]))
    up_in = low_back(matmul(normed2, w_in[0]))
    gate_in = low_back(matmul(normed2, w_in[1]))
    hidden = low(jax.nn.gelu(up_in, approximate=False) * gate_in)
    return h_mid + matmul(hidden, w_down)

def reference(tokens, seq_lengths, w_qkv, w_out, w_in, w_down, gains, cotangent):
    params = (w_qkv.astype(jnp.float32), w_out.astype(jnp.float32), w_in.astype(jnp.float32), w_down.astype(jnp.float32), gains.astype(jnp.float32))
    inputs = tokens.astype(jnp.float32).reshape(N_FSDP, GROUP, D)
    cots = cotangent.astype(jnp.float32).reshape(N_FSDP, GROUP, D)
    lengths = seq_lengths.astype(jnp.int32)

    def whole(weights, rows_all):
        step = jax.checkpoint(lambda rows_g, lens_g: group_layer(weights, rows_g, lens_g))

        def run(carry, pair):
            return (carry, step(pair[0], pair[1]))
        _, outs = lax.scan(run, jnp.zeros((), jnp.float32), (rows_all, lengths))
        return outs
    result, pull = jax.vjp(whole, params, inputs)
    grads, d_inputs = pull(cots)
    return (result.reshape(TOKENS, D).astype(jnp.bfloat16), d_inputs.reshape(TOKENS, D).astype(jnp.bfloat16), grads[0], grads[1], grads[2], grads[3], grads[4])
```

```python
import functools

import jax
import jax.numpy as jnp
from jax import lax
from jax.experimental import pallas as pl
from jax.experimental.pallas import tpu as pltpu
from jax.sharding import PartitionSpec as P

HEAD_DIM = 64
HALF = HEAD_DIM // 2
WIDE = 128
TILE = 256
FAR = -1e30
VMEM_BYTES = 56 * 1024 * 1024
BF16 = jnp.bfloat16
F32 = jnp.float32

NN = (((1,), (0,)), ((), ()))
NT = (((1,), (1,)), ((), ()))
TN = (((0,), (0,)), ((), ()))


def mm(left, right, dims=NN):
    return lax.dot_general(left, right, dims, preferred_element_type=F32)


def positions(lengths, total):
    ends = jnp.cumsum(lengths)
    starts = ends - lengths
    index = jnp.arange(total, dtype=jnp.int32)
    segment = jnp.sum((index[:, None] >= ends[None, :]).astype(jnp.int32), axis=1)
    onehot = segment[:, None] == jnp.arange(lengths.shape[0], dtype=jnp.int32)[None, :]
    first = jnp.sum(jnp.where(onehot, starts[None, :], 0), axis=1)
    last = jnp.sum(jnp.where(onehot, ends[None, :], 0), axis=1)
    return (segment, index - first, first, last)


def rope_tables(place):
    freq = jnp.exp(
        -jnp.log(jnp.float32(160000.0)) * jnp.arange(HALF, dtype=F32) * (2.0 / HEAD_DIM)
    )
    angle = freq[:, None] * place.astype(F32)[None, :]
    return (jnp.cos(angle), jnp.sin(angle))


def pieces_of(row):
    high = row.astype(BF16).astype(F32)
    rest = row - high
    middle = rest.astype(BF16).astype(F32)
    return high, middle, rest - middle


def extend(body, rows):
    rest = WIDE - body.shape[0] - sum(row.shape[0] for row in rows)
    return jnp.concatenate([body, *rows, jnp.zeros((rest, body.shape[1]), F32)], axis=0)


def forward_kernel(
    low_ref, high_ref, tok_ref, gain_ref, seg_ref, cos_ref, sin_ref, wproj_ref, wback_ref,
    normed_ref, query_ref, keys_ref, values_ref, ctx_ref, log_ref, attn_ref,
    nat_ref,
):
    group = tok_ref.shape[0]
    lanes = wback_ref.shape[0]
    heads = lanes // HEAD_DIM
    parts = 8
    count = group // TILE

    @pl.loop(0, count)
    def project(step):
        here = pl.ds(pl.multiple_of(step * TILE, TILE), TILE)
        rows = tok_ref[here, :].astype(F32)
        center = rows - jnp.mean(rows, axis=-1, keepdims=True)
        spread = jnp.mean(center * center, axis=-1, keepdims=True)
        normed = (center * lax.rsqrt(spread + 1e-05) * gain_ref[...]).astype(BF16)
        normed_ref[here, :] = normed
        mixed = mm(wproj_ref[...], normed, NT)
        cosine = cos_ref[:, here]
        sine = sin_ref[:, here]
        segment = seg_ref[:, here]
        same = (segment == lax.broadcasted_iota(jnp.int32, (parts, TILE), 0)).astype(F32)
        ones = jnp.ones((parts, TILE), F32)

        def rotated(top):
            first = mixed[top : top + HALF]
            second = mixed[top + HALF : top + HEAD_DIM]
            return jnp.concatenate(
                [first * cosine - second * sine, second * cosine + first * sine], axis=0
            )

        for head in range(heads):
            top = head * HEAD_DIM
            query = rotated(top) * (HEAD_DIM ** (-0.5))
            query_ref[head, :, here] = extend(query, [(1.0 - same) * FAR]).astype(BF16)
            key = extend(rotated(lanes + top), [same, ones]).astype(BF16)
            keys_ref[head, :, here] = key[:HEAD_DIM]
            nat_ref[head, here, :] = key.T
            value = mixed[2 * lanes + top : 2 * lanes + top + HEAD_DIM]
            values_ref[head, :, here] = value.astype(BF16)

    @pl.loop(0, count)
    def attend(step):
        here = pl.ds(pl.multiple_of(step * TILE, TILE), TILE)

        def inner(at, carry):
            there = pl.ds(pl.multiple_of(at * TILE, TILE), TILE)
            out = []
            for head in range(heads):
                top, total, acc = carry[head]
                scores = mm(nat_ref[head, there, :], query_ref[head, :, here])
                new_top = jnp.maximum(top, jnp.max(scores, axis=0, keepdims=True))
                scale = jnp.exp(top - new_top)
                expo = jnp.exp(scores - new_top)
                total = total * scale + jnp.sum(expo, axis=0, keepdims=True)
                acc = acc * scale + mm(values_ref[head, :, there], expo.astype(BF16))
                out.append((new_top, total, acc))
            return tuple(out)

        start = (
            jnp.full((1, TILE), -jnp.inf, F32),
            jnp.zeros((1, TILE), F32),
            jnp.zeros((HEAD_DIM, TILE), F32),
        )
        done = lax.fori_loop(low_ref[step], high_ref[step], inner, (start,) * heads)
        ctx = jnp.concatenate([acc / total for _, total, acc in done], axis=0).astype(BF16)
        ctx_ref[:, here] = ctx
        logs = [top + jnp.log(total) for top, total, _ in done]
        log_ref[:, here] = jnp.concatenate(
            logs + [jnp.zeros((8 - heads, TILE), F32)], axis=0
        )
        attn_ref[here, :] = mm(ctx.T, wback_ref[...]).astype(BF16)


def backward_kernel(
    low_ref, high_ref, dattn_ref, normed_ref, query_ref, keys_ref, values_ref, ctx_ref, log_ref,
    seg_ref, cos_ref, sin_ref, wproj_ref, wback_ref,
    dnormed_ref, gproj_ref, gback_ref,
    qx_ref, kx_ref, vx_ref, dx_ref, dq_ref, dmix_ref,
):
    group = dattn_ref.shape[0]
    lanes = wback_ref.shape[0]
    heads = lanes // HEAD_DIM
    parts = 8
    count = group // TILE
    scale = HEAD_DIM ** (-0.5)

    @pl.loop(0, count)
    def prepare(step):
        here = pl.ds(pl.multiple_of(step * TILE, TILE), TILE)
        d_ctx = mm(wback_ref[...], dattn_ref[here, :], NT).astype(BF16).astype(F32)
        ctx = ctx_ref[:, here].astype(F32)
        segment = seg_ref[:, here]
        same = (segment == lax.broadcasted_iota(jnp.int32, (parts, TILE), 0)).astype(F32)
        ones = jnp.ones((parts, TILE), F32)
        blank = jnp.zeros((parts - 3, TILE), F32)
        logs = log_ref[:, here]
        for head in range(heads):
            rows = slice(head * HEAD_DIM, (head + 1) * HEAD_DIM)
            delta = -jnp.sum(d_ctx[rows] * ctx[rows], axis=0, keepdims=True)
            dx_ref[head, :, here] = extend(d_ctx[rows], [*pieces_of(delta), blank]).astype(BF16)
            log = -logs[head : head + 1]
            query = query_ref[head, : HEAD_DIM + parts, here].astype(F32)
            qx_ref[head, :, here] = extend(query, [*pieces_of(log), blank]).astype(BF16)
            key = keys_ref[head, :, here].astype(F32)
            kx_ref[head, here, :] = extend(key, [same, ones]).astype(BF16).T
            value = values_ref[head, :, here].astype(F32)
            vx_ref[head, here, :] = extend(value, [ones]).astype(BF16).T
            dq_ref[head, :, here] = jnp.zeros((HEAD_DIM, TILE), F32)

    def turned_back(grad, where):
        cosine = cos_ref[:, where]
        sine = sin_ref[:, where]
        first = grad[:HALF]
        second = grad[HALF:]
        return jnp.concatenate(
            [first * cosine + second * sine, second * cosine - first * sine], axis=0
        ).astype(BF16)

    @pl.loop(0, count)
    def attend(step):
        here = pl.ds(pl.multiple_of(step * TILE, TILE), TILE)

        def inner(at, carry):
            there = pl.ds(pl.multiple_of(at * TILE, TILE), TILE)
            out = []
            for head in range(heads):
                d_key, d_value = carry[head]
                query = qx_ref[head, :, there]
                d_out = dx_ref[head, :, there]
                probs = jnp.exp(mm(kx_ref[head, here, :], query))
                d_probs = mm(vx_ref[head, here, :], d_out)
                d_scores = (probs * d_probs).astype(BF16)
                d_value = d_value + mm(d_out[:HEAD_DIM], probs.astype(BF16), NT)
                d_key = d_key + mm(query[:HEAD_DIM], d_scores, NT)
                dq_ref[head, :, there] += mm(keys_ref[head, :, here], d_scores)
                out.append((d_key, d_value))
            return tuple(out)

        zero = jnp.zeros((HEAD_DIM, TILE), F32)
        done = lax.fori_loop(low_ref[step], high_ref[step], inner, ((zero, zero),) * heads)
        for head in range(heads):
            top = head * HEAD_DIM
            d_key, d_value = done[head]
            dmix_ref[lanes + top : lanes + top + HEAD_DIM, here] = turned_back(d_key, here)
            dmix_ref[2 * lanes + top : 2 * lanes + top + HEAD_DIM, here] = d_value.astype(BF16)

    @pl.loop(0, count)
    def finish(step):
        here = pl.ds(pl.multiple_of(step * TILE, TILE), TILE)
        for head in range(heads):
            top = head * HEAD_DIM
            dmix_ref[top : top + HEAD_DIM, here] = turned_back(dq_ref[head, :, here] * scale, here)
        dnormed_ref[here, :] = mm(dmix_ref[:, here].T, wproj_ref[...]).astype(BF16)

    width = normed_ref.shape[1]
    columns = WIDE
    gback = mm(ctx_ref[...], dattn_ref[...])
    gback_ref[...] = gback.astype(BF16)

    @pl.loop(0, 3)
    def weights(step):
        rows = pl.ds(pl.multiple_of(step * lanes, 64), lanes)
        gproj_ref[rows, :] = mm(dmix_ref[rows, :], normed_ref[...]).astype(BF16)


def vmem_spec():
    return pl.BlockSpec(memory_space=pltpu.VMEM)


def smem_spec():
    return pl.BlockSpec(memory_space=pltpu.SMEM)


def attention_forward(low, high, tok, gain, seg, cosine, sine, wproj, wback):
    group, model = tok.shape
    lanes = wback.shape[0]
    heads = lanes // HEAD_DIM
    shape = jax.ShapeDtypeStruct
    return pl.pallas_call(
        forward_kernel,
        out_shape=(
            shape((group, model), BF16),
            shape((heads, WIDE, group), BF16),
            shape((heads, HEAD_DIM, group), BF16),
            shape((heads, HEAD_DIM, group), BF16),
            shape((lanes, group), BF16),
            shape((8, group), F32),
            shape((group, model), BF16),
        ),
        in_specs=[smem_spec()] * 2 + [vmem_spec()] * 7,
        out_specs=[vmem_spec()] * 7,
        scratch_shapes=[pltpu.VMEM((heads, group, WIDE), BF16)],
        compiler_params=pltpu.CompilerParams(vmem_limit_bytes=VMEM_BYTES),
        cost_estimate=pl.CostEstimate(
            flops=2 * group * model * lanes * 4 + 2 * group * group * lanes,
            bytes_accessed=group * model * 8,
            transcendentals=group * group,
        ),
        name="attention_forward",
    )(low, high, tok, gain, seg, cosine, sine, wproj, wback)


def attention_backward(low, high, d_attn, kept, seg, cosine, sine, wproj, wback):
    group, model = d_attn.shape
    lanes = wback.shape[0]
    heads = lanes // HEAD_DIM
    shape = jax.ShapeDtypeStruct
    return pl.pallas_call(
        backward_kernel,
        out_shape=(
            shape((group, model), BF16),
            shape((3 * lanes, model), BF16),
            shape((lanes, model), BF16),
        ),
        in_specs=[smem_spec()] * 2 + [vmem_spec()] * 12,
        out_specs=[vmem_spec()] * 3,
        scratch_shapes=[
            pltpu.VMEM((heads, WIDE, group), BF16),
            pltpu.VMEM((heads, group, WIDE), BF16),
            pltpu.VMEM((heads, group, WIDE), BF16),
            pltpu.VMEM((heads, WIDE, group), BF16),
            pltpu.VMEM((heads, HEAD_DIM, group), F32),
            pltpu.VMEM((3 * lanes, group), BF16),
        ],
        compiler_params=pltpu.CompilerParams(vmem_limit_bytes=VMEM_BYTES),
        cost_estimate=pl.CostEstimate(
            flops=2 * group * model * lanes * 8 + 4 * group * group * lanes,
            bytes_accessed=group * model * 12,
            transcendentals=group * group,
        ),
        name="attention_backward",
    )(low, high, d_attn, *kept, seg, cosine, sine, wproj, wback)


def swap(value, axis, bit):
    size = lax.axis_size(axis)
    return lax.ppermute(value, axis, [(i, i ^ bit) for i in range(size)])


def gather_rows(rows):
    me = lax.axis_index("tp")
    far = swap(rows, "tp", 2)
    near = swap(rows, "tp", 1)
    corner = swap(far, "tp", 1)
    whole = jnp.zeros((4,) + rows.shape, rows.dtype)
    for bit, block in ((0, rows), (1, near), (2, far), (3, corner)):
        whole = lax.dynamic_update_index_in_dim(whole, block, me ^ bit, 0)
    return whole.reshape(4 * rows.shape[0], rows.shape[1])


def scatter_rows(partial):
    me = lax.axis_index("tp")
    chip, core = me // 2, me % 2
    grid = partial.reshape(2, 2, partial.shape[0] // 4, partial.shape[1])
    take = functools.partial(lax.dynamic_index_in_dim, keepdims=False)
    came = swap(take(grid, 1 - core, 1), "tp", 1)
    pair = came.astype(F32) + take(grid, core, 1).astype(F32)
    far = swap(take(pair, 1 - chip, 0).astype(BF16), "tp", 2)
    return far.astype(F32) + take(pair, chip, 0)


def center_rows(values):
    center = values - jnp.mean(values, axis=-1, keepdims=True)
    spread = jnp.mean(center * center, axis=-1, keepdims=True)
    inverse = lax.rsqrt(spread + 1e-05)
    return center * inverse, inverse


def norm_pull(normal, inverse, gain, grad):
    scaled = grad * gain
    mean = jnp.mean(scaled, axis=-1, keepdims=True)
    along = jnp.mean(scaled * normal, axis=-1, keepdims=True)
    return (scaled - mean - normal * along) * inverse


def geglu(up_in, gate_in):
    return jax.nn.gelu(up_in, approximate=False) * gate_in


def shards(tokens, seq_lengths, w_qkv, w_out, w_in, w_down, gains, cotangent):
    rows, model = tokens.shape
    slab = w_qkv.shape[1]
    lanes = w_qkv.shape[2]
    units = w_in.shape[2]
    group = rows * lax.axis_size("tp")
    count = group // TILE

    own_proj = jnp.transpose(w_qkv, (1, 0, 2)).reshape(slab, 3 * lanes)
    own_pair = jnp.transpose(w_in, (1, 0, 2)).reshape(slab, 2 * units)
    first = jnp.concatenate([own_proj, gains.T], axis=1)
    rest = jnp.concatenate([own_pair, w_out.T, w_down.T], axis=1)
    whole_first = lax.all_gather(first, "fsdp", axis=0, tiled=True)
    whole_rest = lax.all_gather(rest, "fsdp", axis=0, tiled=True)
    proj_t = whole_first[:, : 3 * lanes].T
    gain_one = whole_first[:, 3 * lanes].astype(F32)[None, :]
    gain_two = whole_first[:, 3 * lanes + 1].astype(F32)[None, :]
    pair_cat = whole_rest[:, : 2 * units]
    back = whole_rest[:, 2 * units : 2 * units + lanes].T
    last_t = whole_rest[:, 2 * units + lanes :]

    segment, place, seq_first, seq_last = positions(seq_lengths[0], group)
    cosine, sine = rope_tables(place)
    low = seq_first[::TILE] // TILE
    high = (seq_last[TILE - 1 :: TILE] + TILE - 1) // TILE
    seg = segment[None, :]

    full_tok = gather_rows(tokens)
    full_cot = gather_rows(cotangent)
    normed1, query, keys, values, ctx, logs, attn_part = attention_forward(
        low, high, full_tok, gain_one, seg, cosine, sine, proj_t, back
    )
    inputs = tokens.astype(F32)
    h_mid = inputs + scatter_rows(attn_part)
    normal2, inverse2 = center_rows(h_mid)
    full2 = gather_rows((normal2 * gain_two).astype(BF16))
    both = mm(full2, pair_cat)
    up_in = both[:, :units]
    gate_in = both[:, units:]
    hidden = geglu(up_in, gate_in).astype(BF16)
    mlp = scatter_rows(mm(hidden, last_t, NT).astype(BF16))
    output = (h_mid + mlp).astype(BF16)
    d_hid = mm(full_cot, last_t)
    grad_last_t = mm(full_cot, hidden, TN)
    _, geglu_pull = jax.vjp(geglu, up_in, gate_in)
    d_up, d_gate = geglu_pull(d_hid)
    d_both = jnp.concatenate([d_up, d_gate], axis=1).astype(BF16)
    d_normed2 = scatter_rows(mm(d_both, pair_cat, NT).astype(BF16))
    grad_pair_cat = mm(full2, d_both, TN)
    d_mid = cotangent.astype(F32) + norm_pull(normal2, inverse2, gain_two, d_normed2)
    full_d = gather_rows(d_mid.astype(BF16))
    d_part, grad_proj_t, grad_back = attention_backward(
        low, high, full_d, (normed1, query, keys, values, ctx, logs),
        seg, cosine, sine, proj_t, back,
    )
    d_normed1 = scatter_rows(d_part)
    normal1, inverse1 = center_rows(inputs)
    grad_tokens = (d_mid + norm_pull(normal1, inverse1, gain_one, d_normed1)).astype(BF16)

    late = jnp.concatenate([grad_proj_t, grad_back], axis=0).T
    early = jnp.concatenate([grad_pair_cat, grad_last_t], axis=1).astype(BF16)
    own_early = lax.psum_scatter(early, "fsdp", scatter_dimension=0, tiled=True).astype(F32)
    own_late = lax.psum_scatter(late, "fsdp", scatter_dimension=0, tiled=True).astype(F32)
    sum_proj = own_late[:, : 3 * lanes]
    sum_pair = own_early[:, : 2 * units]
    terms = jnp.stack(
        [
            jnp.sum(sum_proj * own_proj.astype(F32), axis=1),
            jnp.sum(sum_pair * own_pair.astype(F32), axis=1),
        ]
    ) / gains.astype(F32)
    terms = terms + swap(terms, "tp", 1)
    grad_gains = terms + swap(terms, "tp", 2)
    grad_qkv = jnp.transpose(sum_proj.reshape(slab, 3, lanes), (1, 0, 2))
    grad_in = jnp.transpose(sum_pair.reshape(slab, 2, units), (1, 0, 2))
    grad_out = own_late[:, 3 * lanes :].T
    grad_down = own_early[:, 2 * units :].T
    return (output, grad_tokens, grad_qkv, grad_out, grad_in, grad_down, grad_gains)


def solution(mesh):
    rows = P(("fsdp", "tp"), None)
    weights = (P(None, "fsdp", "tp"), P("tp", "fsdp"), P(None, "fsdp", "tp"), P("tp", "fsdp"))
    gains = P(None, "fsdp")
    return jax.shard_map(
        shards,
        mesh=mesh,
        in_specs=(rows, P("fsdp", None), *weights, gains, rows),
        out_specs=(rows, rows, *weights, gains),
        check_vma=False,
    )
```

```python
import functools

import jax
import jax.numpy as jnp
from jax import lax
from jax.experimental import pallas as pl
from jax.experimental.pallas import tpu as pltpu
from jax.sharding import PartitionSpec as P

HEAD_DIM = 64
HALF = HEAD_DIM // 2
WIDE = 128
TILE = 256
FAR = -1e30
VMEM_BYTES = 56 * 1024 * 1024
BF16 = jnp.bfloat16
F32 = jnp.float32

NN = (((1,), (0,)), ((), ()))
NT = (((1,), (1,)), ((), ()))
TN = (((0,), (0,)), ((), ()))


def mm(left, right, dims=NN):
    return lax.dot_general(left, right, dims, preferred_element_type=F32)


def positions(lengths, total):
    ends = jnp.cumsum(lengths)
    starts = ends - lengths
    index = jnp.arange(total, dtype=jnp.int32)
    segment = jnp.sum((index[:, None] >= ends[None, :]).astype(jnp.int32), axis=1)
    onehot = segment[:, None] == jnp.arange(lengths.shape[0], dtype=jnp.int32)[None, :]
    first = jnp.sum(jnp.where(onehot, starts[None, :], 0), axis=1)
    last = jnp.sum(jnp.where(onehot, ends[None, :], 0), axis=1)
    return (segment, index - first, first, last)


def rope_tables(place):
    freq = jnp.exp(
        -jnp.log(jnp.float32(160000.0)) * jnp.arange(HALF, dtype=F32) * (2.0 / HEAD_DIM)
    )
    angle = freq[:, None] * place.astype(F32)[None, :]
    return (jnp.cos(angle), jnp.sin(angle))


def pieces_of(row):
    high = row.astype(BF16).astype(F32)
    rest = row - high
    middle = rest.astype(BF16).astype(F32)
    return high, middle, rest - middle


def extend(body, rows):
    rest = WIDE - body.shape[0] - sum(row.shape[0] for row in rows)
    return jnp.concatenate([body, *rows, jnp.zeros((rest, body.shape[1]), F32)], axis=0)


def slot_of(at, me, split):
    return ((at // split) ^ me) * split + at % split


def tile(at):
    return pl.ds(pl.multiple_of(at * TILE, TILE), TILE)


def forward_kernel(blocks, low_ref, high_ref, me_ref, *refs):
    toks = refs[:4]
    seg_ref, cos_ref, sin_ref = refs[4:7]
    shards_in = refs[7 : 7 + blocks]
    normed_ref, query_ref, keys_ref, values_ref, ctx_ref, log_ref, wproj_ref = refs[
        7 + blocks : 14 + blocks
    ]
    nat_ref, flat_ref = refs[14 + blocks :]
    group = normed_ref.shape[0]
    heads = query_ref.shape[0]
    lanes = heads * HEAD_DIM
    parts = 8
    count = group // TILE
    split = count // 4
    slab = flat_ref.shape[0] // blocks
    me = me_ref[0]

    for index in range(blocks):
        place = pl.multiple_of((me_ref[1] ^ index) * slab, slab)
        flat_ref[pl.ds(place, slab), :] = shards_in[index][...]
    wproj_ref[...] = flat_ref[...].T
    gain = wproj_ref[3 * lanes : 3 * lanes + 16, :].astype(F32)[:1]

    for index in range(4):
        for part in range(split):
            slot = index * split + part
            here = slice(slot * TILE, (slot + 1) * TILE)
            there = tile(slot_of(slot, me, split))
            rows = toks[index][part * TILE : (part + 1) * TILE, :].astype(F32)
            center = rows - jnp.mean(rows, axis=-1, keepdims=True)
            spread = jnp.mean(center * center, axis=-1, keepdims=True)
            normed = (center * lax.rsqrt(spread + 1e-05) * gain).astype(BF16)
            normed_ref[here, :] = normed
            mixed = mm(wproj_ref[: 3 * lanes, :], normed, NT)
            cosine = cos_ref[:, there]
            sine = sin_ref[:, there]
            segment = seg_ref[:, there]
            same = (segment == lax.broadcasted_iota(jnp.int32, (parts, TILE), 0)).astype(F32)
            ones = jnp.ones((2 * parts, TILE), F32)

            def rotated(top):
                first = mixed[top : top + HALF]
                second = mixed[top + HALF : top + HEAD_DIM]
                return jnp.concatenate(
                    [first * cosine - second * sine, second * cosine + first * sine], axis=0
                )

            for head in range(heads):
                top = head * HEAD_DIM
                query = rotated(top) * (HEAD_DIM ** (-0.5))
                query_ref[head, :, here] = extend(query, [(1.0 - same) * FAR]).astype(BF16)
                key = extend(rotated(lanes + top), [same, ones[:parts]]).astype(BF16)
                keys_ref[head, :, here] = key[:HEAD_DIM]
                nat_ref[head, here, :] = key.T
                value = mixed[2 * lanes + top : 2 * lanes + top + HEAD_DIM]
                values_ref[head, :, here] = jnp.concatenate([value, ones], axis=0).astype(BF16)

    @pl.loop(0, count)
    def attend(step):
        here = tile(slot_of(step, me, split))

        def highest(at, tops):
            there = tile(slot_of(at, me, split))
            out = []
            for head in range(heads):
                scores = mm(nat_ref[head, there, :], query_ref[head, :, here])
                out.append(jnp.maximum(tops[head], jnp.max(scores, axis=0, keepdims=True)))
            return tuple(out)

        first = jnp.full((1, TILE), -jnp.inf, F32)
        tops = lax.fori_loop(low_ref[step], high_ref[step], highest, (first,) * heads)
        queries = []
        blank = jnp.zeros((parts - 3, TILE), F32)
        for head in range(heads):
            query = query_ref[head, : HEAD_DIM + parts, here].astype(F32)
            queries.append(extend(query, [*pieces_of(-tops[head]), blank]).astype(BF16))

        def inner(at, accs):
            there = tile(slot_of(at, me, split))
            out = []
            for head in range(heads):
                expo = jnp.exp(mm(nat_ref[head, there, :], queries[head]))
                out.append(accs[head] + mm(values_ref[head, :, there], expo.astype(BF16)))
            return tuple(out)

        zero = jnp.zeros((HEAD_DIM + 2 * parts, TILE), F32)
        accs = lax.fori_loop(low_ref[step], high_ref[step], inner, (zero,) * heads)
        totals = [acc[HEAD_DIM : HEAD_DIM + 1] for acc in accs]
        ctx = [acc[:HEAD_DIM] / total for acc, total in zip(accs, totals)]
        ctx_ref[:, here] = jnp.concatenate(ctx, axis=0).astype(BF16)
        logs = [top + jnp.log(total) for top, total in zip(tops, totals)]
        log_ref[:, here] = jnp.concatenate(
            logs + [jnp.zeros((8 - heads, TILE), F32)], axis=0
        )


def backward_kernel(blocks, low_ref, high_ref, me_ref, *refs):
    dattn = refs[:4]
    (
        normed_ref, query_ref, keys_ref, values_ref, ctx_ref, log_ref, wproj_ref,
        seg_ref, cos_ref, sin_ref, wback_ref, dnormed_ref,
    ) = refs[4:16]
    grads = refs[16 : 16 + blocks]
    (
        qx_ref, kx_ref, vx_ref, dx_ref, dq_ref, dmix_ref, all_ref, tall_ref, flat_ref,
    ) = refs[16 + blocks :]
    group = normed_ref.shape[0]
    lanes = wback_ref.shape[0]
    heads = lanes // HEAD_DIM
    parts = 8
    count = group // TILE
    split = count // 4
    slab = flat_ref.shape[0] // blocks
    me = me_ref[0]
    scale = HEAD_DIM ** (-0.5)

    for index in range(4):
        for part in range(split):
            slot = index * split + part
            here = slice(slot * TILE, (slot + 1) * TILE)
            there = tile(slot_of(slot, me, split))
            piece = dattn[index][part * TILE : (part + 1) * TILE, :]
            all_ref[here, :] = piece
            d_ctx = mm(wback_ref[...], piece, NT).astype(BF16).astype(F32)
            ctx = ctx_ref[:, here].astype(F32)
            segment = seg_ref[:, there]
            same = (segment == lax.broadcasted_iota(jnp.int32, (parts, TILE), 0)).astype(F32)
            ones = jnp.ones((parts, TILE), F32)
            blank = jnp.zeros((parts - 3, TILE), F32)
            logs = log_ref[:, here]
            for head in range(heads):
                rows = slice(head * HEAD_DIM, (head + 1) * HEAD_DIM)
                delta = -jnp.sum(d_ctx[rows] * ctx[rows], axis=0, keepdims=True)
                dx_ref[head, :, here] = extend(
                    d_ctx[rows], [*pieces_of(delta), blank]
                ).astype(BF16)
                log = -logs[head : head + 1]
                query = query_ref[head, : HEAD_DIM + parts, here].astype(F32)
                qx_ref[head, :, here] = extend(query, [*pieces_of(log), blank]).astype(BF16)
                key = keys_ref[head, :, here].astype(F32)
                kx_ref[head, here, :] = extend(key, [same, ones]).astype(BF16).T
                value = values_ref[head, :HEAD_DIM, here].astype(F32)
                vx_ref[head, here, :] = extend(value, [ones]).astype(BF16).T
                dq_ref[head, :, here] = jnp.zeros((HEAD_DIM, TILE), F32)

    def turned_back(grad, where):
        cosine = cos_ref[:, where]
        sine = sin_ref[:, where]
        first = grad[:HALF]
        second = grad[HALF:]
        return jnp.concatenate(
            [first * cosine + second * sine, second * cosine - first * sine], axis=0
        ).astype(BF16)

    @pl.loop(0, count)
    def attend(step):
        here = tile(slot_of(step, me, split))

        def inner(at, carry):
            there = tile(slot_of(at, me, split))
            out = []
            for head in range(heads):
                d_key, d_value = carry[head]
                query = qx_ref[head, :, there]
                d_out = dx_ref[head, :, there]
                probs = jnp.exp(mm(kx_ref[head, here, :], query))
                d_probs = mm(vx_ref[head, here, :], d_out)
                d_scores = (probs * d_probs).astype(BF16)
                d_value = d_value + mm(d_out[:HEAD_DIM], probs.astype(BF16), NT)
                d_key = d_key + mm(query[:HEAD_DIM], d_scores, NT)
                dq_ref[head, :, there] += mm(keys_ref[head, :, here], d_scores)
                out.append((d_key, d_value))
            return tuple(out)

        zero = jnp.zeros((HEAD_DIM, TILE), F32)
        done = lax.fori_loop(low_ref[step], high_ref[step], inner, ((zero, zero),) * heads)
        for head in range(heads):
            top = head * HEAD_DIM
            d_key, d_value = done[head]
            turned = turned_back(d_key, tile(step))
            dmix_ref[lanes + top : lanes + top + HEAD_DIM, here] = turned
            dmix_ref[2 * lanes + top : 2 * lanes + top + HEAD_DIM, here] = d_value.astype(BF16)

    for slot in range(count):
        here = slice(slot * TILE, (slot + 1) * TILE)
        there = tile(slot_of(slot, me, split))
        for head in range(heads):
            top = head * HEAD_DIM
            turned = turned_back(dq_ref[head, :, here] * scale, there)
            dmix_ref[top : top + HEAD_DIM, here] = turned
        d_normed = mm(dmix_ref[:, here].T, wproj_ref[: 3 * lanes, :])
        dnormed_ref[here, :] = d_normed.astype(BF16)

    for step in range(3):
        rows = slice(step * lanes, (step + 1) * lanes)
        tall_ref[rows, :] = mm(dmix_ref[rows, :], normed_ref[...]).astype(BF16)
    tall_ref[3 * lanes :, :] = mm(ctx_ref[...], all_ref[...]).astype(BF16)
    flat_ref[...] = tall_ref[...].T
    for index in range(blocks):
        place = pl.multiple_of((me_ref[1] ^ index) * slab, slab)
        grads[index][...] = flat_ref[pl.ds(place, slab), :]


def vmem_spec():
    return pl.BlockSpec(memory_space=pltpu.VMEM)


def smem_spec():
    return pl.BlockSpec(memory_space=pltpu.SMEM)


def attention_forward(low, high, me, toks, seg, cosine, sine, shards_in, lanes):
    rows, model = toks[0].shape
    group = 4 * rows
    heads = lanes // HEAD_DIM
    blocks = len(shards_in)
    width = shards_in[0].shape[1]
    shape = jax.ShapeDtypeStruct
    return pl.pallas_call(
        functools.partial(forward_kernel, blocks),
        out_shape=(
            shape((group, model), BF16),
            shape((heads, WIDE, group), BF16),
            shape((heads, HEAD_DIM, group), BF16),
            shape((heads, HEAD_DIM + 16, group), BF16),
            shape((lanes, group), BF16),
            shape((8, group), F32),
            shape((width, model), BF16),
        ),
        in_specs=[smem_spec()] * 3 + [vmem_spec()] * (7 + blocks),
        out_specs=[vmem_spec()] * 7,
        scratch_shapes=[
            pltpu.VMEM((heads, group, WIDE), BF16),
            pltpu.VMEM((model, width), BF16),
        ],
        compiler_params=pltpu.CompilerParams(vmem_limit_bytes=VMEM_BYTES),
        cost_estimate=pl.CostEstimate(
            flops=2 * group * model * lanes * 4 + 2 * group * group * lanes,
            bytes_accessed=group * model * 8,
            transcendentals=group * group,
        ),
        name="attention_forward",
    )(low, high, me, *toks, seg, cosine, sine, *shards_in)


def attention_backward(blocks, low, high, me, d_attn, kept, seg, cosine, sine, wback):
    rows, model = d_attn[0].shape
    group = 4 * rows
    lanes = wback.shape[0]
    heads = lanes // HEAD_DIM
    shape = jax.ShapeDtypeStruct
    return pl.pallas_call(
        functools.partial(backward_kernel, blocks),
        out_shape=(
            shape((group, model), BF16),
            *[shape((model // blocks, 4 * lanes), BF16) for _ in range(blocks)],
        ),
        in_specs=[smem_spec()] * 3 + [vmem_spec()] * 15,
        out_specs=[vmem_spec()] * (1 + blocks),
        scratch_shapes=[
            pltpu.VMEM((heads, WIDE, group), BF16),
            pltpu.VMEM((heads, group, WIDE), BF16),
            pltpu.VMEM((heads, group, WIDE), BF16),
            pltpu.VMEM((heads, WIDE, group), BF16),
            pltpu.VMEM((heads, HEAD_DIM, group), F32),
            pltpu.VMEM((3 * lanes, group), BF16),
            pltpu.VMEM((group, model), BF16),
            pltpu.VMEM((4 * lanes, model), BF16),
            pltpu.VMEM((model, 4 * lanes), BF16),
        ],
        compiler_params=pltpu.CompilerParams(vmem_limit_bytes=VMEM_BYTES),
        cost_estimate=pl.CostEstimate(
            flops=2 * group * model * lanes * 8 + 4 * group * group * lanes,
            bytes_accessed=group * model * 12,
            transcendentals=group * group,
        ),
        name="attention_backward",
    )(low, high, me, *d_attn, *kept, seg, cosine, sine, wback)


def swap(value, axis, bit):
    size = lax.axis_size(axis)
    return lax.ppermute(value, axis, [(i, i ^ bit) for i in range(size)])


def gather_rows(rows):
    far = swap(rows, "tp", 2)
    return (rows, swap(rows, "tp", 1), far, swap(far, "tp", 1))


def scatter_rows(partial):
    rows = partial.shape[0] // 4
    own, near, far, corner = (partial[k * rows : (k + 1) * rows] for k in range(4))
    far_sum = far.astype(F32) + swap(corner, "tp", 1).astype(F32)
    came = swap(far_sum.astype(BF16), "tp", 2)
    mine = own.astype(F32) + swap(near, "tp", 1).astype(F32)
    return mine + came.astype(F32)


def pair_rows(rows):
    return jnp.concatenate([rows, swap(rows, "tp", 1)], axis=0)


def scatter_pair(partial):
    rows = partial.shape[0] // 2
    came = swap(partial[rows:].astype(BF16), "tp", 1)
    return partial[:rows] + came.astype(F32)


def swaps_over(axis):
    size = lax.axis_size(axis)
    return size <= 8 and size & (size - 1) == 0


def center_rows(values):
    center = values - jnp.mean(values, axis=-1, keepdims=True)
    spread = jnp.mean(center * center, axis=-1, keepdims=True)
    inverse = lax.rsqrt(spread + 1e-05)
    return center * inverse, inverse


def norm_pull(normal, inverse, gain, grad):
    scaled = grad * gain
    mean = jnp.mean(scaled, axis=-1, keepdims=True)
    along = jnp.mean(scaled * normal, axis=-1, keepdims=True)
    return (scaled - mean - normal * along) * inverse


def geglu(up_in, gate_in):
    return jax.nn.gelu(up_in, approximate=False) * gate_in


def shards(tokens, seq_lengths, w_qkv, w_out, w_in, w_down, gains, cotangent):
    rows, model = tokens.shape
    slab = w_qkv.shape[1]
    lanes = w_qkv.shape[2]
    units = w_in.shape[2]
    group = rows * lax.axis_size("tp")
    ring = lax.axis_size("fsdp")
    direct = swaps_over("fsdp")

    own_proj = jnp.transpose(w_qkv, (1, 0, 2)).reshape(slab, 3 * lanes)
    spare = -(3 * lanes + gains.shape[0]) % WIDE
    first = jnp.concatenate([own_proj, gains.T, jnp.zeros((slab, spare), BF16)], axis=1)
    if direct:
        first_parts = [first] + [swap(first, "fsdp", k) for k in range(1, ring)]
        spot = lax.axis_index("fsdp")
    else:
        first_parts = [lax.all_gather(first, "fsdp", axis=0, tiled=True)]
        spot = jnp.int32(0)
    mine = jnp.concatenate([w_in[0], w_in[1], w_down.T], axis=1)
    other = swap(mine, "tp", 2)
    cut = (slice(0, units), slice(units, 2 * units), slice(2 * units, 3 * units))
    rest = jnp.concatenate(
        [part[:, where] for where in cut for part in (mine, other)] + [w_out.T], axis=1
    )
    whole_rest = lax.all_gather(rest, "fsdp", axis=0, tiled=True)
    pair_cat = whole_rest[:, : 4 * units]
    last_t = whole_rest[:, 4 * units : 6 * units]
    back_t = whole_rest[:, 6 * units :]

    segment, place, seq_first, seq_last = positions(seq_lengths[0], group)
    cosine, sine = rope_tables(place)
    low = seq_first[::TILE] // TILE
    high = (seq_last[TILE - 1 :: TILE] + TILE - 1) // TILE
    seg = segment[None, :]
    me = jnp.stack([lax.axis_index("tp"), spot]).astype(jnp.int32)

    toks = gather_rows(tokens)
    cots = pair_rows(cotangent)
    normed1, query, keys, values, ctx, logs, proj_t = attention_forward(
        low, high, me, toks, seg, cosine, sine, first_parts, lanes
    )
    gain_one = proj_t[3 * lanes : 3 * lanes + 1].astype(F32)
    gain_two = proj_t[3 * lanes + 1 : 3 * lanes + 2].astype(F32)
    inputs = tokens.astype(F32)
    attn_part = lax.dot_general(
        ctx, back_t, (((0,), (1,)), ((), ())), preferred_element_type=F32
    ).astype(BF16)
    h_mid = inputs + scatter_rows(attn_part)
    normal2, inverse2 = center_rows(h_mid)
    full2 = pair_rows((normal2 * gain_two).astype(BF16))
    both = mm(full2, pair_cat)
    up_in = both[:, : 2 * units]
    gate_in = both[:, 2 * units :]
    hidden = geglu(up_in, gate_in).astype(BF16)
    d_hid = mm(cots, last_t)
    _, geglu_pull = jax.vjp(geglu, up_in, gate_in)
    d_up, d_gate = geglu_pull(d_hid)
    d_both = jnp.concatenate([d_up, d_gate], axis=1).astype(BF16)
    d_normed2 = scatter_pair(mm(d_both, pair_cat, NT))
    d_mid = cotangent.astype(F32) + norm_pull(normal2, inverse2, gain_two, d_normed2)
    d_attn = gather_rows(d_mid.astype(BF16))

    output = (h_mid + scatter_pair(mm(hidden, last_t, NT))).astype(BF16)
    early = jnp.concatenate(
        [mm(full2, d_both, TN).astype(BF16), mm(cots, hidden, TN).astype(BF16)], axis=1
    )
    sum_early = lax.psum_scatter(early, "fsdp", scatter_dimension=0, tiled=True)
    halves = [
        jnp.concatenate(
            [sum_early[:, (2 * k + side) * units : (2 * k + side + 1) * units] for k in range(3)],
            axis=1,
        )
        for side in range(2)
    ]
    own_early = halves[0].astype(F32) + swap(halves[1], "tp", 2).astype(F32)

    d_part, *late = attention_backward(
        len(first_parts), low, high, me, d_attn,
        (normed1, query, keys, values, ctx, logs, proj_t), seg, cosine, sine, back_t.T,
    )
    if direct:
        own_late = late[0].astype(F32)
        for k in range(1, ring):
            own_late = own_late + swap(late[k], "fsdp", k).astype(F32)
    else:
        own_late = lax.psum_scatter(late[0], "fsdp", scatter_dimension=0, tiled=True).astype(F32)
    d_normed1 = scatter_rows(d_part)
    normal1, inverse1 = center_rows(inputs)
    grad_tokens = (d_mid + norm_pull(normal1, inverse1, gain_one, d_normed1)).astype(BF16)

    sum_proj = own_late[:, : 3 * lanes]
    terms = jnp.stack(
        [
            jnp.sum(sum_proj * own_proj.astype(F32), axis=1),
            jnp.sum(own_early[:, : 2 * units] * mine[:, : 2 * units].astype(F32), axis=1),
        ]
    ) / gains.astype(F32)
    grad_gains = terms + swap(terms, "tp", 1) + swap(terms, "tp", 2) + swap(terms, "tp", 3)
    grad_qkv = jnp.transpose(sum_proj.reshape(slab, 3, lanes), (1, 0, 2))
    grad_in = jnp.stack([own_early[:, :units], own_early[:, units : 2 * units]])
    grad_out = own_late[:, 3 * lanes :].T
    grad_down = own_early[:, 2 * units :].T
    return (output, grad_tokens, grad_qkv, grad_out, grad_in, grad_down, grad_gains)


def solution(mesh):
    rows = P(("fsdp", "tp"), None)
    weights = (P(None, "fsdp", "tp"), P("tp", "fsdp"), P(None, "fsdp", "tp"), P("tp", "fsdp"))
    gains = P(None, "fsdp")
    return jax.shard_map(
        shards,
        mesh=mesh,
        in_specs=(rows, P("fsdp", None), *weights, gains, rows),
        out_specs=(rows, rows, *weights, gains),
        check_vma=False,
    )
```

```python
import functools

import jax
import jax.numpy as jnp
from jax import lax
from jax.experimental import pallas as pl
from jax.experimental.pallas import tpu as pltpu
from jax.sharding import PartitionSpec as P

HEAD_DIM = 64
HALF = HEAD_DIM // 2
WIDE = 128
TILE = 256
FAR = -1e30
VMEM_BYTES = 56 * 1024 * 1024
BF16 = jnp.bfloat16
F32 = jnp.float32

NN = (((1,), (0,)), ((), ()))
NT = (((1,), (1,)), ((), ()))
TN = (((0,), (0,)), ((), ()))


def mm(left, right, dims=NN):
    return lax.dot_general(left, right, dims, preferred_element_type=F32)


def positions(lengths, total):
    ends = jnp.cumsum(lengths)
    starts = ends - lengths
    index = jnp.arange(total, dtype=jnp.int32)
    segment = jnp.sum((index[:, None] >= ends[None, :]).astype(jnp.int32), axis=1)
    onehot = segment[:, None] == jnp.arange(lengths.shape[0], dtype=jnp.int32)[None, :]
    first = jnp.sum(jnp.where(onehot, starts[None, :], 0), axis=1)
    last = jnp.sum(jnp.where(onehot, ends[None, :], 0), axis=1)
    return (segment, index - first, first, last)


def rope_tables(place):
    freq = jnp.exp(
        -jnp.log(jnp.float32(160000.0)) * jnp.arange(HALF, dtype=F32) * (2.0 / HEAD_DIM)
    )
    angle = freq[:, None] * place.astype(F32)[None, :]
    return (jnp.cos(angle), jnp.sin(angle))


def pieces_of(row):
    high = row.astype(BF16).astype(F32)
    rest = row - high
    middle = rest.astype(BF16).astype(F32)
    return high, middle, rest - middle


def extend(body, rows):
    rest = WIDE - body.shape[0] - sum(row.shape[0] for row in rows)
    return jnp.concatenate([body, *rows, jnp.zeros((rest, body.shape[1]), F32)], axis=0)


def slot_of(at, me, split):
    return ((at // split) ^ me) * split + at % split


def tile(at):
    return pl.ds(pl.multiple_of(at * TILE, TILE), TILE)


def place_shards(spot, shards_in, flat_ref):
    if len(shards_in) == 1:
        flat_ref[...] = shards_in[0][...]
        return
    slab = flat_ref.shape[0] // (2 * len(shards_in))
    for index in range(2 * len(shards_in)):
        place = pl.multiple_of((spot ^ index) * slab, slab)
        piece = shards_in[index // 2][index % 2 * slab : (index % 2 + 1) * slab, :]
        flat_ref[pl.ds(place, slab), :] = piece


def forward_kernel(blocks, low_ref, high_ref, me_ref, *refs):
    toks = refs[:4]
    seg_ref, cos_ref, sin_ref = refs[4:7]
    shards_in = refs[7 : 7 + blocks]
    normed_ref, query_ref, keys_ref, values_ref, ctx_ref, log_ref, wproj_ref = refs[
        7 + blocks : 14 + blocks
    ]
    nat_ref, flat_ref = refs[14 + blocks :]
    group = normed_ref.shape[0]
    heads = query_ref.shape[0]
    lanes = heads * HEAD_DIM
    parts = 8
    count = group // TILE
    split = count // 4
    wide = group // 4
    me = me_ref[0]

    place_shards(me_ref[1], shards_in, flat_ref)
    wproj_ref[...] = flat_ref[...].T
    gain = wproj_ref[3 * lanes : 3 * lanes + 16, :].astype(F32)[:1]

    for slot in range(count):
        rows = toks[slot // split][slot % split * TILE : (slot % split + 1) * TILE, :].astype(F32)
        center = rows - jnp.mean(rows, axis=-1, keepdims=True)
        spread = jnp.mean(center * center, axis=-1, keepdims=True)
        normed = (center * lax.rsqrt(spread + 1e-05) * gain).astype(BF16)
        normed_ref[slot * TILE : (slot + 1) * TILE, :] = normed

    def project(slot):
        return mm(wproj_ref[: 3 * lanes, :], normed_ref[slot * TILE : (slot + 1) * TILE, :], NT)

    upcoming = project(0)
    for slot in range(count):
        mixed = upcoming
        if slot + 1 < count:
            upcoming = project(slot + 1)
        here = slice(slot * TILE, (slot + 1) * TILE)
        there = tile(slot_of(slot, me, split))
        cosine = cos_ref[:, there]
        sine = sin_ref[:, there]
        segment = seg_ref[:, there]
        same = (segment == lax.broadcasted_iota(jnp.int32, (parts, TILE), 0)).astype(F32)
        ones = jnp.ones((2 * parts, TILE), F32)

        def rotated(top):
            first = mixed[top : top + HALF]
            second = mixed[top + HALF : top + HEAD_DIM]
            return jnp.concatenate(
                [first * cosine - second * sine, second * cosine + first * sine], axis=0
            )

        keys = []
        for head in range(heads):
            top = head * HEAD_DIM
            query = rotated(top) * (HEAD_DIM ** (-0.5))
            query_ref[head, :, here] = extend(query, [(1.0 - same) * FAR]).astype(BF16)
            keys.append(extend(rotated(lanes + top), [same, ones[:parts]]).astype(BF16))
            keys_ref[head, :, here] = keys[head][:HEAD_DIM]
            value = mixed[2 * lanes + top : 2 * lanes + top + HEAD_DIM]
            values_ref[head, :, here] = jnp.concatenate([value, ones], axis=0).astype(BF16)
        for head in range(heads):
            nat_ref[head, here, :] = keys[head].T

    every = range(heads)

    @pl.loop(0, 4)
    def attend(step):
        here = pl.ds(pl.multiple_of((step ^ me) * wide, wide), wide)

        def inner(at, carry):
            there = tile(slot_of(at, me, split))
            tops, accs = carry
            scores = [mm(nat_ref[h, there, :], query_ref[h, :, here]) for h in every]
            new = [jnp.maximum(tops[h], jnp.max(scores[h], axis=0, keepdims=True)) for h in every]
            expo = [jnp.exp(scores[h] - new[h]).astype(BF16) for h in every]
            scale = [jnp.exp(tops[h] - new[h]) for h in every]
            accs = [
                accs[h] * scale[h] + mm(values_ref[h, :, there], expo[h]) for h in every
            ]
            return new, accs

        start = (
            [jnp.full((1, wide), -jnp.inf, F32) for _ in every],
            [jnp.zeros((HEAD_DIM + 2 * parts, wide), F32) for _ in every],
        )
        tops, accs = lax.fori_loop(low_ref[step], high_ref[step], inner, start)
        totals = [acc[HEAD_DIM : HEAD_DIM + 1] for acc in accs]
        ctx = [acc[:HEAD_DIM] / total for acc, total in zip(accs, totals)]
        ctx_ref[:, here] = jnp.concatenate(ctx, axis=0).astype(BF16)
        logs = [top + jnp.log(total) for top, total in zip(tops, totals)]
        log_ref[:, here] = jnp.concatenate(
            logs + [jnp.zeros((8 - heads, wide), F32)], axis=0
        )


def backward_kernel(ring, low_ref, high_ref, me_ref, *refs):
    dattn = refs[:4]
    (
        normed_ref, query_ref, keys_ref, values_ref, ctx_ref, log_ref, wproj_ref,
        seg_ref, cos_ref, sin_ref, wback_ref, dnormed_ref,
    ) = refs[4:16]
    grads = refs[16:-9]
    qx_ref, kx_ref, vx_ref, dx_ref, dq_ref, dmix_ref, all_ref, tall_ref, flat_ref = refs[-9:]
    group = normed_ref.shape[0]
    lanes = wback_ref.shape[0]
    heads = lanes // HEAD_DIM
    parts = 8
    count = group // TILE
    split = count // 4
    me = me_ref[0]
    scale = HEAD_DIM ** (-0.5)
    every = range(heads)

    def pull_context(slot):
        piece = dattn[slot // split][slot % split * TILE : (slot % split + 1) * TILE, :]
        all_ref[slot * TILE : (slot + 1) * TILE, :] = piece
        return mm(wback_ref[...], piece, NT)

    upcoming = pull_context(0)
    for slot in range(count):
        here = slice(slot * TILE, (slot + 1) * TILE)
        there = tile(slot_of(slot, me, split))
        d_ctx = upcoming.astype(BF16).astype(F32)
        if slot + 1 < count:
            upcoming = pull_context(slot + 1)
        ctx = ctx_ref[:, here].astype(F32)
        segment = seg_ref[:, there]
        same = (segment == lax.broadcasted_iota(jnp.int32, (parts, TILE), 0)).astype(F32)
        ones = jnp.ones((parts, TILE), F32)
        blank = jnp.zeros((parts - 3, TILE), F32)
        logs = log_ref[:, here]
        natural = []
        for head in every:
            rows = slice(head * HEAD_DIM, (head + 1) * HEAD_DIM)
            delta = -jnp.sum(d_ctx[rows] * ctx[rows], axis=0, keepdims=True)
            dx_ref[head, :, here] = extend(d_ctx[rows], [*pieces_of(delta), blank]).astype(BF16)
            log = -logs[head : head + 1]
            query = query_ref[head, : HEAD_DIM + parts, here].astype(F32)
            qx_ref[head, :, here] = extend(query, [*pieces_of(log), blank]).astype(BF16)
            key = keys_ref[head, :, here].astype(F32)
            value = values_ref[head, :HEAD_DIM, here].astype(F32)
            natural.append(
                (extend(key, [same, ones]).astype(BF16), extend(value, [ones]).astype(BF16))
            )
            dq_ref[head, :, here] = jnp.zeros((HEAD_DIM, TILE), F32)
        for head in every:
            kx_ref[head, here, :] = natural[head][0].T
            vx_ref[head, here, :] = natural[head][1].T

    def turned_back(grad, where):
        cosine = cos_ref[:, where]
        sine = sin_ref[:, where]
        first = grad[:HALF]
        second = grad[HALF:]
        return jnp.concatenate(
            [first * cosine + second * sine, second * cosine - first * sine], axis=0
        ).astype(BF16)

    @pl.loop(0, count)
    def attend(step):
        here = tile(slot_of(step, me, split))

        def inner(at, carry):
            there = tile(slot_of(at, me, split))
            d_keys, d_values = carry
            scores = [mm(kx_ref[h, here, :], qx_ref[h, :, there]) for h in every]
            d_probs = [mm(vx_ref[h, here, :], dx_ref[h, :, there]) for h in every]
            probs = [jnp.exp(score) for score in scores]
            d_scores = [(probs[h] * d_probs[h]).astype(BF16) for h in every]
            low_probs = [prob.astype(BF16) for prob in probs]
            d_values = [
                d_values[h] + mm(dx_ref[h, :HEAD_DIM, there], low_probs[h], NT) for h in every
            ]
            d_keys = [
                d_keys[h] + mm(qx_ref[h, :HEAD_DIM, there], d_scores[h], NT) for h in every
            ]
            for h in every:
                dq_ref[h, :, there] += mm(keys_ref[h, :, here], d_scores[h])
            return d_keys, d_values

        zero = [jnp.zeros((HEAD_DIM, TILE), F32) for _ in every]
        d_keys, d_values = lax.fori_loop(low_ref[step], high_ref[step], inner, (zero, zero))
        for head in every:
            top = head * HEAD_DIM
            turned = turned_back(d_keys[head], tile(step))
            dmix_ref[lanes + top : lanes + top + HEAD_DIM, here] = turned
            d_value = d_values[head].astype(BF16)
            dmix_ref[2 * lanes + top : 2 * lanes + top + HEAD_DIM, here] = d_value

    for slot in range(count):
        here = slice(slot * TILE, (slot + 1) * TILE)
        there = tile(slot_of(slot, me, split))
        for head in every:
            top = head * HEAD_DIM
            turned = turned_back(dq_ref[head, :, here] * scale, there)
            dmix_ref[top : top + HEAD_DIM, here] = turned

    for step in range(3):
        rows = slice(step * lanes, (step + 1) * lanes)
        tall_ref[rows, :] = mm(dmix_ref[rows, :], normed_ref[...]).astype(BF16)
    tall_ref[3 * lanes :, :] = mm(ctx_ref[...], all_ref[...]).astype(BF16)
    flat_ref[...] = tall_ref[...].T
    if len(grads) == 1:
        grads[0][...] = flat_ref[...]
    else:
        slab = flat_ref.shape[0] // ring
        for index in range(ring):
            place = pl.multiple_of((me_ref[1] ^ index) * slab, slab)
            target = slice(index // 2 * slab, (index // 2 + 1) * slab)
            grads[index % 2][target, :] = flat_ref[pl.ds(place, slab), :]

    for slot in range(count):
        here = slice(slot * TILE, (slot + 1) * TILE)
        d_normed = mm(dmix_ref[:, here].T, wproj_ref[: 3 * lanes, :])
        dnormed_ref[here, :] = d_normed.astype(BF16)


def vmem_spec():
    return pl.BlockSpec(memory_space=pltpu.VMEM)


def smem_spec():
    return pl.BlockSpec(memory_space=pltpu.SMEM)


def attention_forward(low, high, me, toks, seg, cosine, sine, shards_in, lanes):
    rows, model = toks[0].shape
    group = 4 * rows
    heads = lanes // HEAD_DIM
    blocks = len(shards_in)
    width = shards_in[0].shape[1]
    shape = jax.ShapeDtypeStruct
    return pl.pallas_call(
        functools.partial(forward_kernel, blocks),
        out_shape=(
            shape((group, model), BF16),
            shape((heads, WIDE, group), BF16),
            shape((heads, HEAD_DIM, group), BF16),
            shape((heads, HEAD_DIM + 16, group), BF16),
            shape((lanes, group), BF16),
            shape((8, group), F32),
            shape((width, model), BF16),
        ),
        in_specs=[smem_spec()] * 3 + [vmem_spec()] * (7 + blocks),
        out_specs=[vmem_spec()] * 7,
        scratch_shapes=[
            pltpu.VMEM((heads, group, WIDE), BF16),
            pltpu.VMEM((model, width), BF16),
        ],
        compiler_params=pltpu.CompilerParams(vmem_limit_bytes=VMEM_BYTES),
        cost_estimate=pl.CostEstimate(
            flops=2 * group * model * lanes * 4 + 2 * group * group * lanes,
            bytes_accessed=group * model * 8,
            transcendentals=group * group,
        ),
        name="attention_forward",
    )(low, high, me, *toks, seg, cosine, sine, *shards_in)


def attention_backward(ring, direct, low, high, me, d_attn, kept, seg, cosine, sine, wback):
    rows, model = d_attn[0].shape
    group = 4 * rows
    lanes = wback.shape[0]
    heads = lanes // HEAD_DIM
    shape = jax.ShapeDtypeStruct
    outs = 2 if direct else 1
    return pl.pallas_call(
        functools.partial(backward_kernel, ring),
        out_shape=(
            shape((group, model), BF16),
            *[shape((model // outs, 4 * lanes), BF16) for _ in range(outs)],
        ),
        in_specs=[smem_spec()] * 3 + [vmem_spec()] * 15,
        out_specs=[vmem_spec()] * (1 + outs),
        scratch_shapes=[
            pltpu.VMEM((heads, WIDE, group), BF16),
            pltpu.VMEM((heads, group, WIDE), BF16),
            pltpu.VMEM((heads, group, WIDE), BF16),
            pltpu.VMEM((heads, WIDE, group), BF16),
            pltpu.VMEM((heads, HEAD_DIM, group), F32),
            pltpu.VMEM((3 * lanes, group), BF16),
            pltpu.VMEM((group, model), BF16),
            pltpu.VMEM((4 * lanes, model), BF16),
            pltpu.VMEM((model, 4 * lanes), BF16),
        ],
        compiler_params=pltpu.CompilerParams(vmem_limit_bytes=VMEM_BYTES),
        cost_estimate=pl.CostEstimate(
            flops=2 * group * model * lanes * 8 + 4 * group * group * lanes,
            bytes_accessed=group * model * 12,
            transcendentals=group * group,
        ),
        name="attention_backward",
    )(low, high, me, *d_attn, *kept, seg, cosine, sine, wback)


def swap(value, axis, bit):
    size = lax.axis_size(axis)
    return lax.ppermute(value, axis, [(i, i ^ bit) for i in range(size)])


def gather_rows(rows):
    far = swap(rows, "tp", 2)
    return (rows, swap(rows, "tp", 1), far, swap(far, "tp", 1))


def scatter_rows(partial):
    rows = partial.shape[0] // 4
    own, near, far, corner = (partial[k * rows : (k + 1) * rows] for k in range(4))
    far_sum = far.astype(F32) + swap(corner, "tp", 1).astype(F32)
    came = swap(far_sum.astype(BF16), "tp", 2)
    mine = own.astype(F32) + swap(near, "tp", 1).astype(F32)
    return mine + came.astype(F32)


def pair_rows(rows):
    return jnp.concatenate([rows, swap(rows, "tp", 1)], axis=0)


def scatter_pair(partial):
    rows = partial.shape[0] // 2
    came = swap(partial[rows:].astype(BF16), "tp", 1)
    return partial[:rows] + came.astype(F32)


def swaps_over(axis):
    size = lax.axis_size(axis)
    return size in (2, 4, 8)


def gather_slabs(slab):
    duo = jnp.concatenate([slab, swap(slab, "fsdp", 1)], axis=0)
    return [duo] + [swap(duo, "fsdp", bit) for bit in range(2, lax.axis_size("fsdp"), 2)]


def pair_slabs(keep, send):
    return (keep.astype(F32) + swap(send, "fsdp", 1).astype(F32)).astype(BF16)


def scatter_slabs(sums):
    ring = lax.axis_size("fsdp")
    slab = 2 * sums.shape[0] // ring
    own = sums[:slab].astype(F32)
    for at in range(1, ring // 2):
        own = own + swap(sums[at * slab : (at + 1) * slab], "fsdp", 2 * at).astype(F32)
    return own


def after(value, *others):
    return lax.optimization_barrier((value, *others))[0]


def center_rows(values):
    center = values - jnp.mean(values, axis=-1, keepdims=True)
    spread = jnp.mean(center * center, axis=-1, keepdims=True)
    inverse = lax.rsqrt(spread + 1e-05)
    return center * inverse, inverse


def norm_pull(normal, inverse, gain, grad):
    scaled = grad * gain
    mean = jnp.mean(scaled, axis=-1, keepdims=True)
    along = jnp.mean(scaled * normal, axis=-1, keepdims=True)
    return (scaled - mean - normal * along) * inverse


def geglu(up_in, gate_in):
    return jax.nn.gelu(up_in, approximate=False) * gate_in


def shards(tokens, seq_lengths, w_qkv, w_out, w_in, w_down, gains, cotangent):
    rows, model = tokens.shape
    slab = w_qkv.shape[1]
    lanes = w_qkv.shape[2]
    units = w_in.shape[2]
    group = rows * lax.axis_size("tp")
    ring = lax.axis_size("fsdp")
    direct = swaps_over("fsdp")
    at_fsdp = lax.axis_index("fsdp")

    own_proj = jnp.transpose(w_qkv, (1, 0, 2)).reshape(slab, 3 * lanes)
    spare = -(3 * lanes + gains.shape[0]) % WIDE
    first = jnp.concatenate([own_proj, gains.T, jnp.zeros((slab, spare), BF16)], axis=1)
    mine = jnp.concatenate([w_in[0], w_in[1], w_down.T], axis=1)
    other = swap(mine, "tp", 2)
    cut = (slice(0, units), slice(units, 2 * units), slice(2 * units, 3 * units))
    rest = jnp.concatenate([part[:, where] for where in cut for part in (mine, other)], axis=1)
    toks = gather_rows(tokens)
    if direct:
        first_parts = gather_slabs(first)
        out_parts = gather_slabs(after(w_out.T, first_parts[-1]))
        rest = after(rest, first_parts[-1])
        back_t = jnp.zeros((model, lanes), BF16)
        for index in range(ring):
            piece = out_parts[index // 2][index % 2 * slab : (index % 2 + 1) * slab]
            back_t = lax.dynamic_update_slice_in_dim(back_t, piece, (at_fsdp ^ index) * slab, 0)
    else:
        first_parts = [lax.all_gather(first, "fsdp", axis=0, tiled=True)]
        back_t = lax.all_gather(w_out.T, "fsdp", axis=0, tiled=True)
    whole_rest = lax.all_gather(rest, "fsdp", axis=0, tiled=True)
    pair_cat = whole_rest[:, : 4 * units]
    last_t = whole_rest[:, 4 * units :]

    segment, place, seq_first, seq_last = positions(seq_lengths[0], group)
    cosine, sine = rope_tables(place)
    low = seq_first[::TILE] // TILE
    high = (seq_last[TILE - 1 :: TILE] + TILE - 1) // TILE
    low_wide = seq_first[::rows] // TILE
    high_wide = (seq_last[rows - 1 :: rows] + TILE - 1) // TILE
    seg = segment[None, :]
    me = jnp.stack([lax.axis_index("tp"), at_fsdp]).astype(jnp.int32)

    normed1, query, keys, values, ctx, logs, proj_t = attention_forward(
        low_wide, high_wide, me, toks, seg, cosine, sine, first_parts, lanes
    )
    gain_one = proj_t[3 * lanes : 3 * lanes + 1].astype(F32)
    gain_two = proj_t[3 * lanes + 1 : 3 * lanes + 2].astype(F32)
    inputs = tokens.astype(F32)
    attn_part = lax.dot_general(
        ctx, back_t, (((0,), (1,)), ((), ())), preferred_element_type=F32
    ).astype(BF16)
    cots = pair_rows(cotangent)
    h_mid = inputs + scatter_rows(attn_part)
    normal2, inverse2 = center_rows(h_mid)
    full2 = pair_rows((normal2 * gain_two).astype(BF16))
    both = mm(full2, pair_cat)
    up_in = both[:, : 2 * units]
    gate_in = both[:, 2 * units :]
    hidden = geglu(up_in, gate_in).astype(BF16)
    d_hid = mm(cots, last_t)
    _, geglu_pull = jax.vjp(geglu, up_in, gate_in)
    d_up, d_gate = geglu_pull(d_hid)
    d_both = jnp.concatenate([d_up, d_gate], axis=1).astype(BF16)
    d_normed2 = scatter_pair(mm(d_both, pair_cat, NT))
    d_mid = cotangent.astype(F32) + norm_pull(normal2, inverse2, gain_two, d_normed2)
    d_low = d_mid.astype(BF16)
    d_attn = gather_rows(d_low)

    hidden = after(hidden, d_low)
    output = (h_mid + scatter_pair(mm(hidden, last_t, NT))).astype(BF16)
    early = jnp.concatenate(
        [
            mm(after(full2, d_low), d_both, TN).astype(BF16),
            mm(cots, hidden, TN).astype(BF16),
        ],
        axis=1,
    )
    if direct:
        grid = early.reshape(ring // 2, 2, slab, early.shape[1])
        take = functools.partial(lax.dynamic_index_in_dim, keepdims=False)
        keep, send = (take(grid, (at_fsdp & 1) ^ side, 1) for side in range(2))
        sums = pair_slabs(keep, send)
        sums = [take(sums, (at_fsdp >> 1) ^ at, 0) for at in range(ring // 2)]
        sum_early = scatter_slabs(jnp.concatenate(sums, axis=0))
    else:
        sum_early = lax.psum_scatter(early, "fsdp", scatter_dimension=0, tiled=True)

    d_part, *late = attention_backward(
        ring, direct, low, high, me, d_attn,
        (normed1, query, keys, values, ctx, logs, proj_t), seg, cosine, sine, back_t.T,
    )
    halves = [
        jnp.concatenate(
            [sum_early[:, (2 * k + side) * units : (2 * k + side + 1) * units] for k in range(3)],
            axis=1,
        )
        for side in range(2)
    ]
    own_early = halves[0].astype(F32) + swap(halves[1].astype(BF16), "tp", 2).astype(F32)
    if direct:
        own_late = scatter_slabs(pair_slabs(*late))
    else:
        own_late = lax.psum_scatter(late[0], "fsdp", scatter_dimension=0, tiled=True).astype(F32)
    d_normed1 = scatter_rows(d_part)
    normal1, inverse1 = center_rows(inputs)
    grad_tokens = (d_mid + norm_pull(normal1, inverse1, gain_one, d_normed1)).astype(BF16)

    sum_proj = own_late[:, : 3 * lanes]
    terms = jnp.stack(
        [
            jnp.sum(sum_proj * own_proj.astype(F32), axis=1),
            jnp.sum(own_early[:, : 2 * units] * mine[:, : 2 * units].astype(F32), axis=1),
        ]
    ) / gains.astype(F32)
    grad_gains = terms + swap(terms, "tp", 1) + swap(terms, "tp", 2) + swap(terms, "tp", 3)
    grad_qkv = jnp.transpose(sum_proj.reshape(slab, 3, lanes), (1, 0, 2))
    grad_in = jnp.stack([own_early[:, :units], own_early[:, units : 2 * units]])
    grad_out = own_late[:, 3 * lanes :].T
    grad_down = own_early[:, 2 * units :].T
    return (output, grad_tokens, grad_qkv, grad_out, grad_in, grad_down, grad_gains)


def solution(mesh):
    rows = P(("fsdp", "tp"), None)
    weights = (P(None, "fsdp", "tp"), P("tp", "fsdp"), P(None, "fsdp", "tp"), P("tp", "fsdp"))
    gains = P(None, "fsdp")
    return jax.shard_map(
        shards,
        mesh=mesh,
        in_specs=(rows, P("fsdp", None), *weights, gains, rows),
        out_specs=(rows, rows, *weights, gains),
        check_vma=False,
    )
```

```python
import functools

import jax
import jax.numpy as jnp
from jax import lax
from jax.experimental import pallas as pl
from jax.experimental.pallas import tpu as pltpu
from jax.sharding import PartitionSpec as P

HEAD_DIM = 64
HALF = HEAD_DIM // 2
WIDE = 128
TILE = 256
FAR = -1e30
VMEM_BYTES = 56 * 1024 * 1024
BF16 = jnp.bfloat16
F32 = jnp.float32

NN = (((1,), (0,)), ((), ()))
NT = (((1,), (1,)), ((), ()))
TN = (((0,), (0,)), ((), ()))


def mm(left, right, dims=NN):
    return lax.dot_general(left, right, dims, preferred_element_type=F32)


def positions(lengths, total):
    ends = jnp.cumsum(lengths)
    starts = ends - lengths
    index = jnp.arange(total, dtype=jnp.int32)
    segment = jnp.sum((index[:, None] >= ends[None, :]).astype(jnp.int32), axis=1)
    onehot = segment[:, None] == jnp.arange(lengths.shape[0], dtype=jnp.int32)[None, :]
    first = jnp.sum(jnp.where(onehot, starts[None, :], 0), axis=1)
    last = jnp.sum(jnp.where(onehot, ends[None, :], 0), axis=1)
    return (segment, index - first, first, last)


def rope_tables(place):
    freq = jnp.exp(
        -jnp.log(jnp.float32(160000.0)) * jnp.arange(HALF, dtype=F32) * (2.0 / HEAD_DIM)
    )
    angle = freq[:, None] * place.astype(F32)[None, :]
    return (jnp.cos(angle), jnp.sin(angle))


def pieces_of(row):
    high = row.astype(BF16).astype(F32)
    rest = row - high
    middle = rest.astype(BF16).astype(F32)
    return high, middle, rest - middle


def extend(body, rows):
    rest = WIDE - body.shape[0] - sum(row.shape[0] for row in rows)
    return jnp.concatenate([body, *rows, jnp.zeros((rest, body.shape[1]), F32)], axis=0)


def slot_of(at, me, split):
    return ((at // split) ^ me) * split + at % split


def tile(at):
    return pl.ds(pl.multiple_of(at * TILE, TILE), TILE)


def place_shards(spot, shards_in, flat_ref):
    slab = shards_in[0].shape[0]
    for index, shard in enumerate(shards_in):
        place = pl.multiple_of((spot ^ index) * slab, slab)
        flat_ref[pl.ds(place, slab), :] = shard[...]


def store_slabs(spot, ring, flat_ref, outs):
    if len(outs) == 1:
        outs[0][...] = flat_ref[...]
        return
    slab = flat_ref.shape[0] // ring
    for index in range(ring):
        place = pl.multiple_of((spot ^ index) * slab, slab)
        target = slice(index // 2 * slab, (index // 2 + 1) * slab)
        outs[index % 2][target, :] = flat_ref[pl.ds(place, slab), :]


def forward_kernel(blocks, low_ref, high_ref, me_ref, *refs):
    toks = refs[:4]
    seg_ref, cos_ref, sin_ref = refs[4:7]
    shards_in = refs[7 : 7 + blocks]
    normed_ref, query_ref, keys_ref, values_ref, ctx_ref, log_ref, wproj_ref = refs[
        7 + blocks : 14 + blocks
    ]
    attns = refs[14 + blocks : 18 + blocks]
    nat_ref, flat_ref, part_ref = refs[18 + blocks :]
    group = normed_ref.shape[0]
    heads = query_ref.shape[0]
    lanes = heads * HEAD_DIM
    parts = 8
    count = group // TILE
    split = count // 4
    wide = group // 4
    me = me_ref[0]

    place_shards(me_ref[1] if blocks > 1 else 0, shards_in, flat_ref)
    wproj_ref[...] = flat_ref[...].T
    gain = wproj_ref[4 * lanes : 4 * lanes + 16, :].astype(F32)[:1]

    for slot in range(count):
        rows = toks[slot // split][slot % split * TILE : (slot % split + 1) * TILE, :].astype(F32)
        center = rows - jnp.mean(rows, axis=-1, keepdims=True)
        spread = jnp.mean(center * center, axis=-1, keepdims=True)
        normed = (center * lax.rsqrt(spread + 1e-05) * gain).astype(BF16)
        normed_ref[slot * TILE : (slot + 1) * TILE, :] = normed

    def project(slot):
        return mm(wproj_ref[: 3 * lanes, :], normed_ref[slot * TILE : (slot + 1) * TILE, :], NT)

    upcoming = project(0)
    for slot in range(count):
        mixed = upcoming
        if slot + 1 < count:
            upcoming = project(slot + 1)
        here = slice(slot * TILE, (slot + 1) * TILE)
        there = tile(slot_of(slot, me, split))
        cosine = cos_ref[:, there]
        sine = sin_ref[:, there]
        segment = seg_ref[:, there]
        same = (segment == lax.broadcasted_iota(jnp.int32, (parts, TILE), 0)).astype(F32)
        ones = jnp.ones((2 * parts, TILE), F32)

        def rotated(top):
            first = mixed[top : top + HALF]
            second = mixed[top + HALF : top + HEAD_DIM]
            return jnp.concatenate(
                [first * cosine - second * sine, second * cosine + first * sine], axis=0
            )

        keys = []
        for head in range(heads):
            top = head * HEAD_DIM
            query = rotated(top) * (HEAD_DIM ** (-0.5))
            query_ref[head, :, here] = extend(query, [(1.0 - same) * FAR]).astype(BF16)
            keys.append(extend(rotated(lanes + top), [same, ones[:parts]]).astype(BF16))
            keys_ref[head, :, here] = keys[head][:HEAD_DIM]
            value = mixed[2 * lanes + top : 2 * lanes + top + HEAD_DIM]
            values_ref[head, :, here] = jnp.concatenate([value, ones], axis=0).astype(BF16)
        for head in range(heads):
            nat_ref[head, here, :] = keys[head].T

    every = range(heads)

    @pl.loop(0, 4)
    def attend(step):
        here = pl.ds(pl.multiple_of((step ^ me) * wide, wide), wide)

        def inner(at, carry):
            there = tile(slot_of(at, me, split))
            tops, accs = carry
            scores = [mm(nat_ref[h, there, :], query_ref[h, :, here]) for h in every]
            new = [jnp.maximum(tops[h], jnp.max(scores[h], axis=0, keepdims=True)) for h in every]
            expo = [jnp.exp(scores[h] - new[h]).astype(BF16) for h in every]
            scale = [jnp.exp(tops[h] - new[h]) for h in every]
            accs = [
                accs[h] * scale[h] + mm(values_ref[h, :, there], expo[h]) for h in every
            ]
            return new, accs

        start = (
            [jnp.full((1, wide), -jnp.inf, F32) for _ in every],
            [jnp.zeros((HEAD_DIM + 2 * parts, wide), F32) for _ in every],
        )
        tops, accs = lax.fori_loop(low_ref[step], high_ref[step], inner, start)
        totals = [acc[HEAD_DIM : HEAD_DIM + 1] for acc in accs]
        ctx = [acc[:HEAD_DIM] / total for acc, total in zip(accs, totals)]
        ctx = jnp.concatenate(ctx, axis=0).astype(BF16)
        ctx_ref[:, here] = ctx
        logs = [top + jnp.log(total) for top, total in zip(tops, totals)]
        log_ref[:, here] = jnp.concatenate(
            logs + [jnp.zeros((8 - heads, wide), F32)], axis=0
        )
        part_ref[here, :] = mm(ctx.T, wproj_ref[3 * lanes : 4 * lanes, :]).astype(BF16)

    for index in range(4):
        attns[index][...] = part_ref[index * wide : (index + 1) * wide, :]


def backward_kernel(ring, low_ref, high_ref, me_ref, *refs):
    dattn = refs[:4]
    (
        normed_ref, query_ref, keys_ref, values_ref, ctx_ref, log_ref, wproj_ref,
        seg_ref, cos_ref, sin_ref,
    ) = refs[4:14]
    dnormeds = refs[14:18]
    grads = refs[18:-9]
    qx_ref, kx_ref, vx_ref, dx_ref, dq_ref, dmix_ref, all_ref, tall_ref, flat_ref = refs[-9:]
    group = normed_ref.shape[0]
    lanes = ctx_ref.shape[0]
    heads = lanes // HEAD_DIM
    parts = 8
    count = group // TILE
    split = count // 4
    me = me_ref[0]
    scale = HEAD_DIM ** (-0.5)
    every = range(heads)

    def pull_context(slot):
        piece = dattn[slot // split][slot % split * TILE : (slot % split + 1) * TILE, :]
        all_ref[slot * TILE : (slot + 1) * TILE, :] = piece
        return mm(wproj_ref[3 * lanes : 4 * lanes, :], piece, NT)

    upcoming = pull_context(0)
    for slot in range(count):
        here = slice(slot * TILE, (slot + 1) * TILE)
        there = tile(slot_of(slot, me, split))
        d_ctx = upcoming.astype(BF16).astype(F32)
        if slot + 1 < count:
            upcoming = pull_context(slot + 1)
        ctx = ctx_ref[:, here].astype(F32)
        segment = seg_ref[:, there]
        same = (segment == lax.broadcasted_iota(jnp.int32, (parts, TILE), 0)).astype(F32)
        ones = jnp.ones((parts, TILE), F32)
        blank = jnp.zeros((parts - 3, TILE), F32)
        logs = log_ref[:, here]
        natural = []
        for head in every:
            rows = slice(head * HEAD_DIM, (head + 1) * HEAD_DIM)
            delta = -jnp.sum(d_ctx[rows] * ctx[rows], axis=0, keepdims=True)
            dx_ref[head, :, here] = extend(d_ctx[rows], [*pieces_of(delta), blank]).astype(BF16)
            log = -logs[head : head + 1]
            query = query_ref[head, : HEAD_DIM + parts, here].astype(F32)
            qx_ref[head, :, here] = extend(query, [*pieces_of(log), blank]).astype(BF16)
            key = keys_ref[head, :, here].astype(F32)
            value = values_ref[head, :HEAD_DIM, here].astype(F32)
            natural.append(
                (extend(key, [same, ones]).astype(BF16), extend(value, [ones]).astype(BF16))
            )
            dq_ref[head, :, here] = jnp.zeros((HEAD_DIM, TILE), F32)
        for head in every:
            kx_ref[head, here, :] = natural[head][0].T
            vx_ref[head, here, :] = natural[head][1].T

    def turned_back(grad, where):
        cosine = cos_ref[:, where]
        sine = sin_ref[:, where]
        first = grad[:HALF]
        second = grad[HALF:]
        return jnp.concatenate(
            [first * cosine + second * sine, second * cosine - first * sine], axis=0
        ).astype(BF16)

    @pl.loop(0, count)
    def attend(step):
        here = tile(slot_of(step, me, split))

        def inner(at, carry):
            there = tile(slot_of(at, me, split))
            d_keys, d_values = carry
            scores = [mm(kx_ref[h, here, :], qx_ref[h, :, there]) for h in every]
            d_probs = [mm(vx_ref[h, here, :], dx_ref[h, :, there]) for h in every]
            probs = [jnp.exp(score) for score in scores]
            d_scores = [(probs[h] * d_probs[h]).astype(BF16) for h in every]
            low_probs = [prob.astype(BF16) for prob in probs]
            d_values = [
                d_values[h] + mm(dx_ref[h, :HEAD_DIM, there], low_probs[h], NT) for h in every
            ]
            d_keys = [
                d_keys[h] + mm(qx_ref[h, :HEAD_DIM, there], d_scores[h], NT) for h in every
            ]
            for h in every:
                dq_ref[h, :, there] += mm(keys_ref[h, :, here], d_scores[h])
            return d_keys, d_values

        zero = [jnp.zeros((HEAD_DIM, TILE), F32) for _ in every]
        d_keys, d_values = lax.fori_loop(low_ref[step], high_ref[step], inner, (zero, zero))
        for head in every:
            top = head * HEAD_DIM
            turned = turned_back(d_keys[head], tile(step))
            dmix_ref[lanes + top : lanes + top + HEAD_DIM, here] = turned
            d_value = d_values[head].astype(BF16)
            dmix_ref[2 * lanes + top : 2 * lanes + top + HEAD_DIM, here] = d_value

    for slot in range(count):
        here = slice(slot * TILE, (slot + 1) * TILE)
        there = tile(slot_of(slot, me, split))
        for head in every:
            top = head * HEAD_DIM
            turned = turned_back(dq_ref[head, :, here] * scale, there)
            dmix_ref[top : top + HEAD_DIM, here] = turned

    for step in range(3):
        rows = slice(step * lanes, (step + 1) * lanes)
        tall_ref[rows, :] = mm(dmix_ref[rows, :], normed_ref[...]).astype(BF16)
    tall_ref[3 * lanes :, :] = mm(ctx_ref[...], all_ref[...]).astype(BF16)
    flat_ref[...] = tall_ref[...].T
    store_slabs(me_ref[1], ring, flat_ref, grads)

    for slot in range(count):
        here = slice(slot * TILE, (slot + 1) * TILE)
        d_normed = mm(dmix_ref[:, here].T, wproj_ref[: 3 * lanes, :])
        inside = slice(slot % split * TILE, (slot % split + 1) * TILE)
        dnormeds[slot // split][inside, :] = d_normed.astype(BF16)


def mlp_kernel(ring, me_ref, *refs):
    own_ref, near_ref, cot_ref, cot_near_ref, rest_ref = refs[:5]
    d_own_ref, d_near_ref, hidden_ref, d_both_ref = refs[5:9]
    grads = refs[9:-3]
    pair_ref, cots_ref, flat_ref = refs[-3:]
    rows, model = own_ref.shape
    wide = hidden_ref.shape[1]
    units = flat_ref.shape[1]
    count = 2 * rows // TILE
    half = count // 2

    def start(slot):
        inside = slice(slot % half * TILE, (slot % half + 1) * TILE)
        normed = (own_ref, near_ref)[slot // half][inside, :]
        cot = (cot_ref, cot_near_ref)[slot // half][inside, :]
        cots_ref[:, slot * TILE : (slot + 1) * TILE] = cot.T
        return mm(normed, rest_ref[:, : 2 * wide]), mm(cot, rest_ref[:, 2 * wide :])

    upcoming = start(0)
    pair_ref[...] = rest_ref[:, : 2 * wide].T
    for slot in range(count):
        both, d_hid = upcoming
        if slot + 1 < count:
            upcoming = start(slot + 1)
        here = slice(slot * TILE, (slot + 1) * TILE)
        inside = slice(slot % half * TILE, (slot % half + 1) * TILE)
        up_in = both[:, :wide]
        gate_in = both[:, wide:]
        share = 0.5 + 0.5 * lax.erf(up_in * (0.5**0.5))
        slope = share + up_in * jnp.exp(-0.5 * up_in * up_in) * 0.3989422804014327
        curve = up_in * share
        hidden_ref[here, :] = (curve * gate_in).astype(BF16)
        d_up = (d_hid * gate_in * slope).astype(BF16)
        d_gate = (d_hid * curve).astype(BF16)
        d_both_ref[here, :wide] = d_up
        d_both_ref[here, wide:] = d_gate
        d_normed = mm(d_up, pair_ref[:wide, :]) + mm(d_gate, pair_ref[wide:, :])
        (d_own_ref, d_near_ref)[slot // half][inside, :] = d_normed.astype(BF16)
    flat_ref[...] = mm(cots_ref[...], hidden_ref[...])[:, :units].astype(BF16)
    store_slabs(me_ref[0], ring, flat_ref, grads)


def mlp_late_kernel(ring, me_ref, *refs):
    own_ref, near_ref, hidden_ref, d_both_ref, rest_ref, out_own_ref, out_near_ref = refs[:7]
    grads = refs[7:-3]
    rows_ref, last_ref, flat_ref = refs[-3:]
    rows = own_ref.shape[0]
    wide = hidden_ref.shape[1]
    units = flat_ref.shape[1] // 2
    rows_ref[:, :rows] = own_ref[...].T
    rows_ref[:, rows:] = near_ref[...].T
    grad = mm(rows_ref[...], d_both_ref[...]).astype(BF16)
    flat_ref[...] = jnp.concatenate([grad[:, :units], grad[:, wide : wide + units]], axis=1)
    store_slabs(me_ref[0], ring, flat_ref, grads)
    last_ref[...] = rest_ref[:, 2 * wide :].T
    out_own_ref[...] = mm(hidden_ref[:rows, :], last_ref[...]).astype(BF16)
    out_near_ref[...] = mm(hidden_ref[rows:, :], last_ref[...]).astype(BF16)


def vmem_spec():
    return pl.BlockSpec(memory_space=pltpu.VMEM)


def smem_spec():
    return pl.BlockSpec(memory_space=pltpu.SMEM)


def attention_forward(low, high, me, toks, seg, cosine, sine, shards_in, lanes):
    rows, model = toks[0].shape
    group = 4 * rows
    heads = lanes // HEAD_DIM
    blocks = len(shards_in)
    width = shards_in[0].shape[1]
    shape = jax.ShapeDtypeStruct
    return pl.pallas_call(
        functools.partial(forward_kernel, blocks),
        out_shape=(
            shape((group, model), BF16),
            shape((heads, WIDE, group), BF16),
            shape((heads, HEAD_DIM, group), BF16),
            shape((heads, HEAD_DIM + 16, group), BF16),
            shape((lanes, group), BF16),
            shape((8, group), F32),
            shape((width, model), BF16),
            *[shape((rows, model), BF16) for _ in range(4)],
        ),
        in_specs=[smem_spec()] * 3 + [vmem_spec()] * (7 + blocks),
        out_specs=[vmem_spec()] * 11,
        scratch_shapes=[
            pltpu.VMEM((heads, group, WIDE), BF16),
            pltpu.VMEM((model, width), BF16),
            pltpu.VMEM((group, model), BF16),
        ],
        compiler_params=pltpu.CompilerParams(vmem_limit_bytes=VMEM_BYTES),
        cost_estimate=pl.CostEstimate(
            flops=2 * group * model * lanes * 4 + 2 * group * group * lanes,
            bytes_accessed=group * model * 8,
            transcendentals=group * group,
        ),
        name="attention_forward",
    )(low, high, me, *toks, seg, cosine, sine, *shards_in)


def attention_backward(ring, direct, low, high, me, d_attn, kept, seg, cosine, sine):
    rows, model = d_attn[0].shape
    group = 4 * rows
    lanes = kept[4].shape[0]
    heads = lanes // HEAD_DIM
    shape = jax.ShapeDtypeStruct
    outs = 2 if direct else 1
    return pl.pallas_call(
        functools.partial(backward_kernel, ring),
        out_shape=(
            *[shape((rows, model), BF16) for _ in range(4)],
            *[shape((model // outs, 4 * lanes), BF16) for _ in range(outs)],
        ),
        in_specs=[smem_spec()] * 3 + [vmem_spec()] * 14,
        out_specs=[vmem_spec()] * (4 + outs),
        scratch_shapes=[
            pltpu.VMEM((heads, WIDE, group), BF16),
            pltpu.VMEM((heads, group, WIDE), BF16),
            pltpu.VMEM((heads, group, WIDE), BF16),
            pltpu.VMEM((heads, WIDE, group), BF16),
            pltpu.VMEM((heads, HEAD_DIM, group), F32),
            pltpu.VMEM((3 * lanes, group), BF16),
            pltpu.VMEM((group, model), BF16),
            pltpu.VMEM((4 * lanes, model), BF16),
            pltpu.VMEM((model, 4 * lanes), BF16),
        ],
        compiler_params=pltpu.CompilerParams(vmem_limit_bytes=VMEM_BYTES),
        cost_estimate=pl.CostEstimate(
            flops=2 * group * model * lanes * 64,
            bytes_accessed=group * model * 12,
            transcendentals=group * group,
        ),
        name="attention_backward",
    )(low, high, me, *d_attn, *kept, seg, cosine, sine)


def mlp(ring, direct, spot, rows_in, cots, rest, units):
    rows, model = rows_in[0].shape
    wide = rest.shape[1] // 3
    outs = 2 if direct else 1
    shape = jax.ShapeDtypeStruct
    return pl.pallas_call(
        functools.partial(mlp_kernel, ring),
        out_shape=(
            shape((rows, model), BF16),
            shape((rows, model), BF16),
            shape((2 * rows, wide), BF16),
            shape((2 * rows, 2 * wide), BF16),
            *[shape((model // outs, units), BF16) for _ in range(outs)],
        ),
        in_specs=[smem_spec()] + [vmem_spec()] * 5,
        out_specs=[vmem_spec()] * (4 + outs),
        scratch_shapes=[
            pltpu.VMEM((2 * wide, model), BF16),
            pltpu.VMEM((model, 2 * rows), BF16),
            pltpu.VMEM((model, units), BF16),
        ],
        compiler_params=pltpu.CompilerParams(vmem_limit_bytes=VMEM_BYTES),
        cost_estimate=pl.CostEstimate(
            flops=24 * rows * model * wide, bytes_accessed=rows * model * 16, transcendentals=0
        ),
        name="mlp",
    )(spot, *rows_in, *cots, rest)


def mlp_late(ring, direct, spot, rows_in, hidden, d_both, rest, units):
    rows, model = rows_in[0].shape
    wide = hidden.shape[1]
    outs = 2 if direct else 1
    shape = jax.ShapeDtypeStruct
    return pl.pallas_call(
        functools.partial(mlp_late_kernel, ring),
        out_shape=(
            shape((rows, model), BF16),
            shape((rows, model), BF16),
            *[shape((model // outs, 2 * units), BF16) for _ in range(outs)],
        ),
        in_specs=[smem_spec()] + [vmem_spec()] * 5,
        out_specs=[vmem_spec()] * (2 + outs),
        scratch_shapes=[
            pltpu.VMEM((model, 2 * rows), BF16),
            pltpu.VMEM((wide, model), BF16),
            pltpu.VMEM((model, 2 * units), BF16),
        ],
        compiler_params=pltpu.CompilerParams(vmem_limit_bytes=VMEM_BYTES),
        cost_estimate=pl.CostEstimate(
            flops=12 * rows * model * wide, bytes_accessed=rows * model * 16, transcendentals=0
        ),
        name="mlp_late",
    )(spot, *rows_in, hidden, d_both, rest)


def swap(value, axis, bit):
    size = lax.axis_size(axis)
    return lax.ppermute(value, axis, [(i, i ^ bit) for i in range(size)])


def gather_rows(rows):
    far = swap(rows, "tp", 2)
    return (rows, swap(rows, "tp", 1), far, swap(far, "tp", 1))


def scatter_rows(own, near, far, corner):
    far_sum = (far.astype(F32) + swap(corner, "tp", 1).astype(F32)).astype(BF16)
    came = swap(far_sum, "tp", 2)
    mine = own.astype(F32) + swap(near, "tp", 1).astype(F32)
    return mine + came.astype(F32), far_sum


def pair_sum(own, near):
    return own.astype(F32) + swap(near, "tp", 1).astype(F32)


def swaps_over(axis):
    size = lax.axis_size(axis)
    return size in (2, 4, 8)


def gather_slabs(slab):
    evens = [slab] + [swap(slab, "fsdp", bit) for bit in range(2, lax.axis_size("fsdp"), 2)]
    return [block for even in evens for block in (even, swap(even, "fsdp", 1))]


def pair_slabs(keep, send):
    return (keep.astype(F32) + swap(send, "fsdp", 1).astype(F32)).astype(BF16)


def scatter_slabs(sums):
    ring = lax.axis_size("fsdp")
    slab = 2 * sums.shape[0] // ring
    own = sums[:slab].astype(F32)
    for at in range(1, ring // 2):
        own = own + swap(sums[at * slab : (at + 1) * slab], "fsdp", 2 * at).astype(F32)
    return own


def after(value, *others):
    return lax.optimization_barrier((value, *others))[0]


def center_rows(values):
    center = values - jnp.mean(values, axis=-1, keepdims=True)
    spread = jnp.mean(center * center, axis=-1, keepdims=True)
    inverse = lax.rsqrt(spread + 1e-05)
    return center * inverse, inverse


def norm_pull(normal, inverse, gain, grad):
    scaled = grad * gain
    mean = jnp.mean(scaled, axis=-1, keepdims=True)
    along = jnp.mean(scaled * normal, axis=-1, keepdims=True)
    return (scaled - mean - normal * along) * inverse


def shards(tokens, seq_lengths, w_qkv, w_out, w_in, w_down, gains, cotangent):
    rows, model = tokens.shape
    slab = w_qkv.shape[1]
    lanes = w_qkv.shape[2]
    units = w_in.shape[2]
    group = rows * lax.axis_size("tp")
    ring = lax.axis_size("fsdp")
    direct = swaps_over("fsdp")
    at_fsdp = lax.axis_index("fsdp")

    own_proj = jnp.transpose(w_qkv, (1, 0, 2)).reshape(slab, 3 * lanes)
    spare = -(4 * lanes + gains.shape[0]) % WIDE
    first = jnp.concatenate(
        [own_proj, w_out.T, gains.T, jnp.zeros((slab, spare), BF16)], axis=1
    )
    far = swap(tokens, "tp", 2)
    near = swap(tokens, "tp", 1)
    if direct:
        first_parts = gather_slabs(after(first, near))
    else:
        first_parts = [lax.all_gather(first, "fsdp", axis=0, tiled=True)]
    corner = swap(after(far, *first_parts), "tp", 1)
    toks = (tokens, near, far, corner)
    mine = jnp.concatenate([w_in[0], w_in[1], w_down.T], axis=1)
    other = swap(after(mine, far), "tp", 2)
    spare = jnp.zeros((slab, -2 * units % WIDE), BF16)
    rest = jnp.concatenate(
        [
            part
            for k in range(3)
            for part in (mine[:, k * units : (k + 1) * units], other[:, k * units : (k + 1) * units], spare)
        ],
        axis=1,
    )
    rest = after(rest, *first_parts)
    whole_rest = lax.all_gather(rest, "fsdp", axis=0, tiled=True)

    segment, place, seq_first, seq_last = positions(seq_lengths[0], group)
    cosine, sine = rope_tables(place)
    low = seq_first[::TILE] // TILE
    high = (seq_last[TILE - 1 :: TILE] + TILE - 1) // TILE
    low_wide = seq_first[::rows] // TILE
    high_wide = (seq_last[rows - 1 :: rows] + TILE - 1) // TILE
    seg = segment[None, :]
    me = jnp.stack([lax.axis_index("tp"), at_fsdp]).astype(jnp.int32)

    *kept, proj_t, own, near, far, corner = attention_forward(
        low_wide, high_wide, me, toks, seg, cosine, sine, first_parts, lanes
    )
    gain_one = proj_t[4 * lanes : 4 * lanes + 1].astype(F32)
    gain_two = proj_t[4 * lanes + 1 : 4 * lanes + 2].astype(F32)
    inputs = tokens.astype(F32)
    cots = (cotangent, swap(cotangent, "tp", 1))
    h_mid = inputs + scatter_rows(own, near, far, corner)[0]
    normal2, inverse2 = center_rows(h_mid)
    normed2 = (normal2 * gain_two).astype(BF16)
    full2 = (normed2, swap(normed2, "tp", 1))
    spot = me[1:]
    d_own, d_near, hidden, d_both, *last_halves = mlp(
        ring, direct, spot, full2, cots, whole_rest, 2 * units
    )
    d_normed2 = pair_sum(d_own, d_near)
    d_mid = cotangent.astype(F32) + norm_pull(normal2, inverse2, gain_two, d_normed2)
    d_low = d_mid.astype(BF16)
    d_attn = gather_rows(d_low)

    out_own, out_near, *pair_halves = mlp_late(
        ring, direct, spot, full2, after(hidden, d_attn[1]), d_both, whole_rest, 2 * units
    )
    output = (h_mid + pair_sum(out_own, out_near)).astype(BF16)
    if direct:
        pair_sums = pair_slabs(*pair_halves).reshape(ring // 2, slab, 4 * units)
        last_sums = pair_slabs(*last_halves).reshape(ring // 2, slab, 2 * units)
        sums = [
            jnp.concatenate([pair_sums[at], last_sums[at]], axis=1) for at in range(ring // 2)
        ]
        d_attn, sums, output = lax.optimization_barrier((d_attn, sums, output))
        sums = [sums[0]] + [swap(sums[at], "fsdp", 2 * at) for at in range(1, ring // 2)]

    d_parts = attention_backward(
        ring, direct, low, high, me, d_attn, (*kept, proj_t), seg, cosine, sine
    )
    if direct:
        d_parts, sums = lax.optimization_barrier((d_parts, sums))
    late = d_parts[4:]
    d_normed1, far_sum = scatter_rows(*d_parts[:4])
    if direct:
        sum_early = after(sums[0], far_sum).astype(F32)
        for at in range(1, ring // 2):
            sum_early = sum_early + sums[at].astype(F32)
        own_late = scatter_slabs(pair_slabs(after(late[0], far_sum), late[1]))
    else:
        early = jnp.concatenate([pair_halves[0], last_halves[0]], axis=1)
        sum_early = lax.psum_scatter(early, "fsdp", scatter_dimension=0, tiled=True)
        own_late = lax.psum_scatter(late[0], "fsdp", scatter_dimension=0, tiled=True).astype(F32)
    halves = [
        jnp.concatenate(
            [sum_early[:, (2 * k + side) * units : (2 * k + side + 1) * units] for k in range(3)],
            axis=1,
        )
        for side in range(2)
    ]
    own_early = halves[0].astype(F32) + swap(halves[1].astype(BF16), "tp", 2).astype(F32)
    normal1, inverse1 = center_rows(inputs)
    grad_tokens = (d_mid + norm_pull(normal1, inverse1, gain_one, d_normed1)).astype(BF16)

    sum_proj = own_late[:, : 3 * lanes]
    terms = jnp.stack(
        [
            jnp.sum(sum_proj * own_proj.astype(F32), axis=1),
            jnp.sum(own_early[:, : 2 * units] * mine[:, : 2 * units].astype(F32), axis=1),
        ]
    ) / gains.astype(F32)
    grad_gains = terms + swap(terms, "tp", 1) + swap(terms, "tp", 2) + swap(terms, "tp", 3)
    grad_qkv = jnp.transpose(sum_proj.reshape(slab, 3, lanes), (1, 0, 2))
    grad_in = jnp.stack([own_early[:, :units], own_early[:, units : 2 * units]])
    grad_out = own_late[:, 3 * lanes :].T
    grad_down = own_early[:, 2 * units :].T
    return (output, grad_tokens, grad_qkv, grad_out, grad_in, grad_down, grad_gains)


def solution(mesh):
    rows = P(("fsdp", "tp"), None)
    weights = (P(None, "fsdp", "tp"), P("tp", "fsdp"), P(None, "fsdp", "tp"), P("tp", "fsdp"))
    gains = P(None, "fsdp")
    return jax.shard_map(
        shards,
        mesh=mesh,
        in_specs=(rows, P("fsdp", None), *weights, gains, rows),
        out_specs=(rows, rows, *weights, gains),
        check_vma=False,
    )
```

```python
import functools

import jax
import jax.numpy as jnp
from jax import lax
from jax.experimental import pallas as pl
from jax.experimental.pallas import tpu as pltpu
from jax.sharding import PartitionSpec as P

HEAD_DIM = 64
HALF = HEAD_DIM // 2
WIDE = 128
TILE = 256
FAR = -1e30
VMEM_BYTES = 56 * 1024 * 1024
BF16 = jnp.bfloat16
F32 = jnp.float32

NN = (((1,), (0,)), ((), ()))
NT = (((1,), (1,)), ((), ()))
TN = (((0,), (0,)), ((), ()))


def mm(left, right, dims=NN):
    return lax.dot_general(left, right, dims, preferred_element_type=F32)


def positions(lengths, total):
    ends = jnp.cumsum(lengths)
    starts = ends - lengths
    index = jnp.arange(total, dtype=jnp.int32)
    segment = jnp.sum((index[:, None] >= ends[None, :]).astype(jnp.int32), axis=1)
    onehot = segment[:, None] == jnp.arange(lengths.shape[0], dtype=jnp.int32)[None, :]
    first = jnp.sum(jnp.where(onehot, starts[None, :], 0), axis=1)
    last = jnp.sum(jnp.where(onehot, ends[None, :], 0), axis=1)
    return (segment, index - first, first, last)


def rope_tables(place):
    freq = jnp.exp(
        -jnp.log(jnp.float32(160000.0)) * jnp.arange(HALF, dtype=F32) * (2.0 / HEAD_DIM)
    )
    angle = freq[:, None] * place.astype(F32)[None, :]
    return (jnp.cos(angle), jnp.sin(angle))


def pieces_of(row):
    high = row.astype(BF16).astype(F32)
    rest = row - high
    middle = rest.astype(BF16).astype(F32)
    return high, middle, rest - middle


def extend(body, rows):
    rest = WIDE - body.shape[0] - sum(row.shape[0] for row in rows)
    return jnp.concatenate([body, *rows, jnp.zeros((rest, body.shape[1]), F32)], axis=0)


def slot_of(at, me, split):
    return ((at // split) ^ me) * split + at % split


def tile(at):
    return pl.ds(pl.multiple_of(at * TILE, TILE), TILE)


def place_shards(spot, shards_in, flat_ref):
    slab = shards_in[0].shape[0]
    for index, shard in enumerate(shards_in):
        place = pl.multiple_of((spot ^ index) * slab, slab)
        flat_ref[pl.ds(place, slab), :] = shard[...]


def store_slabs(spot, ring, flat_ref, outs):
    if len(outs) == 1:
        outs[0][...] = flat_ref[...]
        return
    slab = flat_ref.shape[0] // ring
    for index in range(ring):
        place = pl.multiple_of((spot ^ index) * slab, slab)
        target = slice(index // 2 * slab, (index // 2 + 1) * slab)
        outs[index % 2][target, :] = flat_ref[pl.ds(place, slab), :]


def forward_kernel(blocks, low_ref, high_ref, me_ref, *refs):
    toks = refs[:4]
    seg_ref, cos_ref, sin_ref = refs[4:7]
    shards_in = refs[7 : 7 + blocks]
    normed_ref, query_ref, keys_ref, nat_ref, values_ref, wproj_ref = refs[
        7 + blocks : 13 + blocks
    ]
    attended = refs[13 + blocks : 17 + blocks]
    flat_ref = refs[17 + blocks]
    group = normed_ref.shape[0]
    heads = query_ref.shape[0]
    lanes = heads * HEAD_DIM
    parts = 8
    count = group // TILE
    split = count // 4
    wide = group // 4
    me = me_ref[0]

    place_shards(me_ref[1] if blocks > 1 else 0, shards_in, flat_ref)
    wproj_ref[...] = flat_ref[...].T
    gain = wproj_ref[4 * lanes : 4 * lanes + 16, :].astype(F32)[:1]

    for slot in range(count):
        rows = toks[slot // split][slot % split * TILE : (slot % split + 1) * TILE, :].astype(F32)
        center = rows - jnp.mean(rows, axis=-1, keepdims=True)
        spread = jnp.mean(center * center, axis=-1, keepdims=True)
        normed = (center * lax.rsqrt(spread + 1e-05) * gain).astype(BF16)
        normed_ref[slot * TILE : (slot + 1) * TILE, :] = normed

    def project(slot):
        return mm(wproj_ref[: 3 * lanes, :], normed_ref[slot * TILE : (slot + 1) * TILE, :], NT)

    upcoming = project(0)
    for slot in range(count):
        mixed = upcoming
        if slot + 1 < count:
            upcoming = project(slot + 1)
        here = slice(slot * TILE, (slot + 1) * TILE)
        there = tile(slot_of(slot, me, split))
        cosine = cos_ref[:, there]
        sine = sin_ref[:, there]
        segment = seg_ref[:, there]
        same = (segment == lax.broadcasted_iota(jnp.int32, (parts, TILE), 0)).astype(F32)
        ones = jnp.ones((2 * parts, TILE), F32)

        def rotated(top):
            first = mixed[top : top + HALF]
            second = mixed[top + HALF : top + HEAD_DIM]
            return jnp.concatenate(
                [first * cosine - second * sine, second * cosine + first * sine], axis=0
            )

        keys = []
        for head in range(heads):
            top = head * HEAD_DIM
            query = rotated(top) * (HEAD_DIM ** (-0.5))
            query_ref[head, :, here] = extend(query, [(1.0 - same) * FAR]).astype(BF16)
            keys.append(extend(rotated(lanes + top), [same, ones[:parts]]).astype(BF16))
            keys_ref[head, :, here] = keys[head][:HEAD_DIM]
            value = mixed[2 * lanes + top : 2 * lanes + top + HEAD_DIM]
            values_ref[head, :, here] = jnp.concatenate([value, ones], axis=0).astype(BF16)
        for head in range(heads):
            nat_ref[head, here, :] = keys[head].T

    attend_slots(
        (2, 3), me, low_ref, high_ref, query_ref, nat_ref, values_ref, wproj_ref, *attended
    )


def forward_own_kernel(low_ref, high_ref, me_ref, query_ref, nat_ref, values_ref, wproj_ref, *outs):
    attend_slots(
        (0, 1), me_ref[0], low_ref, high_ref, query_ref, nat_ref, values_ref, wproj_ref, *outs
    )


def attend_slots(
    slots, me, low_ref, high_ref, query_ref, nat_ref, values_ref, wproj_ref, ctx_ref, log_ref, *attns
):
    heads, _, group = query_ref.shape
    lanes = heads * HEAD_DIM
    parts = 8
    wide = group // 4
    split = wide // TILE
    every = range(heads)

    for index, slot in enumerate(slots):
        step = slot ^ me
        here = slice(slot * wide, (slot + 1) * wide)

        def inner(at, carry):
            there = tile(slot_of(at, me, split))
            tops, accs = carry
            scores = [mm(nat_ref[h, there, :], query_ref[h, :, here]) for h in every]
            new = [jnp.maximum(tops[h], jnp.max(scores[h], axis=0, keepdims=True)) for h in every]
            expo = [jnp.exp(scores[h] - new[h]).astype(BF16) for h in every]
            scale = [jnp.exp(tops[h] - new[h]) for h in every]
            accs = [
                accs[h] * scale[h] + mm(values_ref[h, :, there], expo[h]) for h in every
            ]
            return new, accs

        start = (
            [jnp.full((1, wide), -jnp.inf, F32) for _ in every],
            [jnp.zeros((HEAD_DIM + 2 * parts, wide), F32) for _ in every],
        )
        tops, accs = lax.fori_loop(low_ref[step], high_ref[step], inner, start)
        totals = [acc[HEAD_DIM : HEAD_DIM + 1] for acc in accs]
        ctx = [acc[:HEAD_DIM] / total for acc, total in zip(accs, totals)]
        ctx = jnp.concatenate(ctx, axis=0).astype(BF16)
        where = slice(index * wide, (index + 1) * wide)
        ctx_ref[:, where] = ctx
        logs = [top + jnp.log(total) for top, total in zip(tops, totals)]
        log_ref[:, where] = jnp.concatenate(
            logs + [jnp.zeros((8 - heads, wide), F32)], axis=0
        )
        attns[index][...] = mm(ctx.T, wproj_ref[3 * lanes : 4 * lanes, :]).astype(BF16)


def backward_kernel(ring, low_ref, high_ref, me_ref, *refs):
    dattn = refs[:4]
    normed_ref, query_ref, keys_ref, kx_ref, values_ref, wproj_ref = refs[4:10]
    ctxs = refs[10:14:2]
    log_refs = refs[11:14:2]
    cos_ref, sin_ref = refs[14:16]
    dnormeds = refs[16:20]
    grads = refs[20:-8]
    qx_ref, vx_ref, dx_ref, dq_ref, dmix_ref, all_ref, tall_ref, flat_ref = refs[-8:]
    group = normed_ref.shape[0]
    lanes = ctxs[0].shape[0]
    heads = lanes // HEAD_DIM
    parts = 8
    count = group // TILE
    split = count // 4
    me = me_ref[0]
    scale = HEAD_DIM ** (-0.5)
    every = range(heads)

    def pull_context(slot):
        piece = dattn[slot // split][slot % split * TILE : (slot % split + 1) * TILE, :]
        all_ref[slot * TILE : (slot + 1) * TILE, :] = piece
        return mm(wproj_ref[3 * lanes : 4 * lanes, :], piece, NT)

    upcoming = pull_context(0)
    for slot in range(count):
        here = slice(slot * TILE, (slot + 1) * TILE)
        d_ctx = upcoming.astype(BF16).astype(F32)
        if slot + 1 < count:
            upcoming = pull_context(slot + 1)
        inside = slice(slot % (2 * split) * TILE, (slot % (2 * split) + 1) * TILE)
        ctx = ctxs[slot // (2 * split)][:, inside].astype(F32)
        logs = log_refs[slot // (2 * split)][:, inside]
        ones = jnp.ones((parts, TILE), F32)
        blank = jnp.zeros((parts - 3, TILE), F32)
        natural = []
        for head in every:
            rows = slice(head * HEAD_DIM, (head + 1) * HEAD_DIM)
            delta = -jnp.sum(d_ctx[rows] * ctx[rows], axis=0, keepdims=True)
            dx_ref[head, :, here] = extend(d_ctx[rows], [*pieces_of(delta), blank]).astype(BF16)
            log = -logs[head : head + 1]
            query = query_ref[head, : HEAD_DIM + parts, here].astype(F32)
            qx_ref[head, :, here] = extend(query, [*pieces_of(log), blank]).astype(BF16)
            value = values_ref[head, :HEAD_DIM, here].astype(F32)
            natural.append(extend(value, [ones]).astype(BF16))
            dq_ref[head, :, here] = jnp.zeros((HEAD_DIM, TILE), F32)
        for head in every:
            vx_ref[head, here, :] = natural[head].T

    def turned_back(grad, where):
        cosine = cos_ref[:, where]
        sine = sin_ref[:, where]
        first = grad[:HALF]
        second = grad[HALF:]
        return jnp.concatenate(
            [first * cosine + second * sine, second * cosine - first * sine], axis=0
        ).astype(BF16)

    @pl.loop(0, count)
    def attend(step):
        here = tile(slot_of(step, me, split))

        def inner(at, carry):
            there = tile(slot_of(at, me, split))
            d_keys, d_values = carry
            scores = [mm(kx_ref[h, here, :], qx_ref[h, :, there]) for h in every]
            d_probs = [mm(vx_ref[h, here, :], dx_ref[h, :, there]) for h in every]
            probs = [jnp.exp(score) for score in scores]
            d_scores = [(probs[h] * d_probs[h]).astype(BF16) for h in every]
            low_probs = [prob.astype(BF16) for prob in probs]
            d_values = [
                d_values[h] + mm(dx_ref[h, :HEAD_DIM, there], low_probs[h], NT) for h in every
            ]
            d_keys = [
                d_keys[h] + mm(qx_ref[h, :HEAD_DIM, there], d_scores[h], NT) for h in every
            ]
            for h in every:
                dq_ref[h, :, there] += mm(keys_ref[h, :, here], d_scores[h])
            return d_keys, d_values

        zero = [jnp.zeros((HEAD_DIM, TILE), F32) for _ in every]
        d_keys, d_values = lax.fori_loop(low_ref[step], high_ref[step], inner, (zero, zero))
        for head in every:
            top = head * HEAD_DIM
            turned = turned_back(d_keys[head], tile(step))
            dmix_ref[lanes + top : lanes + top + HEAD_DIM, here] = turned
            d_value = d_values[head].astype(BF16)
            dmix_ref[2 * lanes + top : 2 * lanes + top + HEAD_DIM, here] = d_value

    for slot in range(count):
        here = slice(slot * TILE, (slot + 1) * TILE)
        there = tile(slot_of(slot, me, split))
        for head in every:
            top = head * HEAD_DIM
            turned = turned_back(dq_ref[head, :, here] * scale, there)
            dmix_ref[top : top + HEAD_DIM, here] = turned

    for step in range(3):
        rows = slice(step * lanes, (step + 1) * lanes)
        tall_ref[rows, :] = mm(dmix_ref[rows, :], normed_ref[...]).astype(BF16)
    tall_ref[3 * lanes :, :] = sum(
        mm(ctx[...], all_ref[index * group // 2 : (index + 1) * group // 2, :])
        for index, ctx in enumerate(ctxs)
    ).astype(BF16)
    flat_ref[...] = tall_ref[...].T
    store_slabs(me_ref[1], ring, flat_ref, grads)

    for slot in range(count):
        here = slice(slot * TILE, (slot + 1) * TILE)
        d_normed = mm(dmix_ref[:, here].T, wproj_ref[: 3 * lanes, :])
        inside = slice(slot % split * TILE, (slot % split + 1) * TILE)
        dnormeds[slot // split][inside, :] = d_normed.astype(BF16)


def mlp_kernel(ring, me_ref, *refs):
    own_ref, near_ref, cot_ref, cot_near_ref, rest_ref = refs[:5]
    d_own_ref, d_near_ref, hidden_ref = refs[5:8]
    grads = refs[8:-5]
    pair_ref, rows_ref, cots_ref, d_both_ref, flat_ref = refs[-5:]
    rows, model = own_ref.shape
    wide = hidden_ref.shape[1]
    units = flat_ref.shape[1] // 3
    count = 2 * rows // TILE
    half = count // 2

    def start(slot):
        inside = slice(slot % half * TILE, (slot % half + 1) * TILE)
        normed = (own_ref, near_ref)[slot // half][inside, :]
        cot = (cot_ref, cot_near_ref)[slot // half][inside, :]
        cots_ref[:, slot * TILE : (slot + 1) * TILE] = cot.T
        rows_ref[:, slot * TILE : (slot + 1) * TILE] = normed.T
        return mm(normed, rest_ref[:, : 2 * wide]), mm(cot, rest_ref[:, 2 * wide :])

    upcoming = start(0)
    pair_ref[...] = rest_ref[:, : 2 * wide].T
    for slot in range(count):
        both, d_hid = upcoming
        if slot + 1 < count:
            upcoming = start(slot + 1)
        here = slice(slot * TILE, (slot + 1) * TILE)
        inside = slice(slot % half * TILE, (slot % half + 1) * TILE)
        up_in = both[:, :wide]
        gate_in = both[:, wide:]
        share = 0.5 + 0.5 * lax.erf(up_in * (0.5**0.5))
        slope = share + up_in * jnp.exp(-0.5 * up_in * up_in) * 0.3989422804014327
        curve = up_in * share
        hidden_ref[here, :] = (curve * gate_in).astype(BF16)
        d_up = (d_hid * gate_in * slope).astype(BF16)
        d_gate = (d_hid * curve).astype(BF16)
        d_both_ref[here, :wide] = d_up
        d_both_ref[here, wide:] = d_gate
        d_normed = mm(d_up, pair_ref[:wide, :]) + mm(d_gate, pair_ref[wide:, :])
        (d_own_ref, d_near_ref)[slot // half][inside, :] = d_normed.astype(BF16)
    grad = mm(rows_ref[...], d_both_ref[...]).astype(BF16)
    last = mm(cots_ref[...], hidden_ref[...]).astype(BF16)
    flat_ref[:, : 2 * units] = jnp.concatenate(
        [grad[:, :units], grad[:, wide : wide + units]], axis=1
    )
    flat_ref[:, 2 * units :] = last[:, :units]
    store_slabs(me_ref[0], ring, flat_ref.at[:, : 2 * units], grads[:2] if len(grads) > 2 else grads[:1])
    if len(grads) == 2:
        grads[1][...] = flat_ref[:, 2 * units :]
    else:
        slab = model // ring
        for index in range(ring):
            place = pl.multiple_of((me_ref[0] ^ index) * slab, slab)
            target = slice(index % 2 * slab, (index % 2 + 1) * slab)
            grads[2 + index // 2][target, :] = flat_ref[pl.ds(place, slab), 2 * units :]


def down_kernel(hidden_ref, rest_ref, own_ref, near_ref, last_ref):
    rows = own_ref.shape[0]
    last_ref[...] = rest_ref[:, 2 * hidden_ref.shape[1] :].T
    own_ref[...] = mm(hidden_ref[:rows, :], last_ref[...]).astype(BF16)
    near_ref[...] = mm(hidden_ref[rows:, :], last_ref[...]).astype(BF16)


def vmem_spec():
    return pl.BlockSpec(memory_space=pltpu.VMEM)


def smem_spec():
    return pl.BlockSpec(memory_space=pltpu.SMEM)


def attention_forward(low, high, me, toks, seg, cosine, sine, shards_in, lanes):
    rows, model = toks[0].shape
    group = 4 * rows
    heads = lanes // HEAD_DIM
    blocks = len(shards_in)
    width = shards_in[0].shape[1]
    shape = jax.ShapeDtypeStruct
    return pl.pallas_call(
        functools.partial(forward_kernel, blocks),
        out_shape=(
            shape((group, model), BF16),
            shape((heads, WIDE, group), BF16),
            shape((heads, HEAD_DIM, group), BF16),
            shape((heads, group, WIDE), BF16),
            shape((heads, HEAD_DIM + 16, group), BF16),
            shape((width, model), BF16),
            shape((lanes, group // 2), BF16),
            shape((8, group // 2), F32),
            *[shape((rows, model), BF16) for _ in range(2)],
        ),
        in_specs=[smem_spec()] * 3 + [vmem_spec()] * (7 + blocks),
        out_specs=[vmem_spec()] * 10,
        scratch_shapes=[pltpu.VMEM((model, width), BF16)],
        compiler_params=pltpu.CompilerParams(vmem_limit_bytes=VMEM_BYTES),
        cost_estimate=pl.CostEstimate(
            flops=group * model * lanes,
            bytes_accessed=group * model,
            transcendentals=0,
        ),
        name="attention_forward",
    )(low, high, me, *toks, seg, cosine, sine, *shards_in)


def attention_forward_own(low, high, me, query, nat, values, proj_t):
    heads, _, group = query.shape
    model = proj_t.shape[1]
    rows = group // 4
    shape = jax.ShapeDtypeStruct
    return pl.pallas_call(
        forward_own_kernel,
        out_shape=(
            shape((heads * HEAD_DIM, group // 2), BF16),
            shape((8, group // 2), F32),
            *[shape((rows, model), BF16) for _ in range(2)],
        ),
        in_specs=[smem_spec()] * 3 + [vmem_spec()] * 4,
        out_specs=[vmem_spec()] * 4,
        compiler_params=pltpu.CompilerParams(vmem_limit_bytes=VMEM_BYTES),
        cost_estimate=pl.CostEstimate(
            flops=group * model * heads * HEAD_DIM,
            bytes_accessed=group * model,
            transcendentals=0,
        ),
        name="attention_forward_own",
    )(low, high, me, query, nat, values, proj_t)


def attention_backward(ring, direct, low, high, me, d_attn, kept, cosine, sine):
    rows, model = d_attn[0].shape
    group = 4 * rows
    lanes = kept[6].shape[0]
    heads = lanes // HEAD_DIM
    shape = jax.ShapeDtypeStruct
    outs = 2 if direct else 1
    return pl.pallas_call(
        functools.partial(backward_kernel, ring),
        out_shape=(
            *[shape((rows, model), BF16) for _ in range(4)],
            *[shape((model // outs, 4 * lanes), BF16) for _ in range(outs)],
        ),
        in_specs=[smem_spec()] * 3 + [vmem_spec()] * 16,
        out_specs=[vmem_spec()] * (4 + outs),
        scratch_shapes=[
            pltpu.VMEM((heads, WIDE, group), BF16),
            pltpu.VMEM((heads, group, WIDE), BF16),
            pltpu.VMEM((heads, WIDE, group), BF16),
            pltpu.VMEM((heads, HEAD_DIM, group), F32),
            pltpu.VMEM((3 * lanes, group), BF16),
            pltpu.VMEM((group, model), BF16),
            pltpu.VMEM((4 * lanes, model), BF16),
            pltpu.VMEM((model, 4 * lanes), BF16),
        ],
        compiler_params=pltpu.CompilerParams(vmem_limit_bytes=VMEM_BYTES),
        cost_estimate=pl.CostEstimate(
            flops=2 * group * model * lanes * 64,
            bytes_accessed=group * model * 12,
            transcendentals=group * group,
        ),
        name="attention_backward",
    )(low, high, me, *d_attn, *kept, cosine, sine)


def mlp(ring, direct, spot, rows_in, cots, rest, units):
    rows, model = rows_in[0].shape
    wide = rest.shape[1] // 3
    outs = 2 if direct else 1
    lasts = ring // 2 if direct else 1
    shape = jax.ShapeDtypeStruct
    return pl.pallas_call(
        functools.partial(mlp_kernel, ring),
        out_shape=(
            shape((rows, model), BF16),
            shape((rows, model), BF16),
            shape((2 * rows, wide), BF16),
            *[shape((model // outs, 2 * units), BF16) for _ in range(outs)],
            *[shape((model // lasts, units), BF16) for _ in range(lasts)],
        ),
        in_specs=[smem_spec()] + [vmem_spec()] * 5,
        out_specs=[vmem_spec()] * (3 + outs + lasts),
        scratch_shapes=[
            pltpu.VMEM((2 * wide, model), BF16),
            pltpu.VMEM((model, 2 * rows), BF16),
            pltpu.VMEM((model, 2 * rows), BF16),
            pltpu.VMEM((2 * rows, 2 * wide), BF16),
            pltpu.VMEM((model, 3 * units), BF16),
        ],
        compiler_params=pltpu.CompilerParams(vmem_limit_bytes=VMEM_BYTES),
        cost_estimate=pl.CostEstimate(
            flops=24 * rows * model * wide, bytes_accessed=rows * model * 16, transcendentals=0
        ),
        name="mlp",
    )(spot, *rows_in, *cots, rest)


def down(hidden, rest):
    rows, wide = hidden.shape
    model = rest.shape[0]
    out = jax.ShapeDtypeStruct((rows // 2, model), BF16)
    return pl.pallas_call(
        down_kernel,
        out_shape=(out, out),
        in_specs=[vmem_spec()] * 2,
        out_specs=[vmem_spec()] * 2,
        scratch_shapes=[pltpu.VMEM((wide, model), BF16)],
        compiler_params=pltpu.CompilerParams(vmem_limit_bytes=VMEM_BYTES),
        cost_estimate=pl.CostEstimate(
            flops=2 * rows * model * wide, bytes_accessed=rows * model * 6, transcendentals=0
        ),
        name="down",
    )(hidden, rest)


def swap(value, axis, bit):
    size = lax.axis_size(axis)
    return lax.ppermute(value, axis, [(i, i ^ bit) for i in range(size)])


def gather_rows(rows):
    far = swap(rows, "tp", 2)
    return (rows, swap(rows, "tp", 1), far, swap(far, "tp", 1))


def sum_far(far, corner):
    return (far.astype(F32) + swap(corner, "tp", 1).astype(F32)).astype(BF16)


def sum_rows(own, near, came):
    return own.astype(F32) + swap(near, "tp", 1).astype(F32) + came.astype(F32)


def pair_sum(own, near):
    return own.astype(F32) + swap(near, "tp", 1).astype(F32)


def swaps_over(axis):
    size = lax.axis_size(axis)
    return size in (2, 4, 8)


def gather_slabs(slab):
    evens = [slab] + [swap(slab, "fsdp", bit) for bit in range(2, lax.axis_size("fsdp"), 2)]
    return [block for even in evens for block in (even, swap(even, "fsdp", 1))]


def pair_slabs(keep, send):
    return (keep.astype(F32) + swap(send, "fsdp", 1).astype(F32)).astype(BF16)


def scatter_slabs(sums):
    ring = lax.axis_size("fsdp")
    slab = 2 * sums.shape[0] // ring
    own = sums[:slab].astype(F32)
    for at in range(1, ring // 2):
        own = own + swap(sums[at * slab : (at + 1) * slab], "fsdp", 2 * at).astype(F32)
    return own


def after(value, *others):
    return lax.optimization_barrier((value, *others))[0]


def center_rows(values):
    center = values - jnp.mean(values, axis=-1, keepdims=True)
    spread = jnp.mean(center * center, axis=-1, keepdims=True)
    inverse = lax.rsqrt(spread + 1e-05)
    return center * inverse, inverse


def norm_pull(normal, inverse, gain, grad):
    scaled = grad * gain
    mean = jnp.mean(scaled, axis=-1, keepdims=True)
    along = jnp.mean(scaled * normal, axis=-1, keepdims=True)
    return (scaled - mean - normal * along) * inverse


def shards(tokens, seq_lengths, w_qkv, w_out, w_in, w_down, gains, cotangent):
    rows, model = tokens.shape
    slab = w_qkv.shape[1]
    lanes = w_qkv.shape[2]
    units = w_in.shape[2]
    group = rows * lax.axis_size("tp")
    ring = lax.axis_size("fsdp")
    direct = swaps_over("fsdp")
    at_fsdp = lax.axis_index("fsdp")

    own_proj = jnp.transpose(w_qkv, (1, 0, 2)).reshape(slab, 3 * lanes)
    spare = -(4 * lanes + gains.shape[0]) % WIDE
    first = jnp.concatenate(
        [own_proj, w_out.T, gains.T, jnp.zeros((slab, spare), BF16)], axis=1
    )
    far = swap(tokens, "tp", 2)
    near = swap(tokens, "tp", 1)
    seq_lengths, w_in, w_down = lax.optimization_barrier((seq_lengths, w_in, w_down, far))[:3]
    if direct:
        first_parts = gather_slabs(after(first, near))
    else:
        first_parts = [lax.all_gather(first, "fsdp", axis=0, tiled=True)]
    mine = jnp.concatenate([w_in[0], w_in[1], w_down.T], axis=1)
    other = swap(mine, "tp", 2)
    spare = jnp.zeros((slab, -2 * units % WIDE), BF16)
    rest = jnp.concatenate(
        [
            part
            for k in range(3)
            for part in (mine[:, k * units : (k + 1) * units], other[:, k * units : (k + 1) * units], spare)
        ],
        axis=1,
    )
    rest = after(rest, *first_parts[::2])
    corner = swap(after(far, rest, *first_parts), "tp", 1)
    toks = (tokens, near, far, corner)
    whole_rest = lax.all_gather(rest, "fsdp", axis=0, tiled=True)

    segment, place, seq_first, seq_last = positions(seq_lengths[0], group)
    cosine, sine = rope_tables(place)
    low = seq_first[::TILE] // TILE
    high = (seq_last[TILE - 1 :: TILE] + TILE - 1) // TILE
    low_wide = seq_first[::rows] // TILE
    high_wide = (seq_last[rows - 1 :: rows] + TILE - 1) // TILE
    seg = segment[None, :]
    me = jnp.stack([lax.axis_index("tp"), at_fsdp]).astype(jnp.int32)

    *kept, proj_t, ctx_far, log_far, far, corner = attention_forward(
        low_wide, high_wide, me, toks, seg, cosine, sine, first_parts, lanes
    )
    far_sum = sum_far(far, corner)
    normed1, query, keys, nat, values = kept
    ctx_own, log_own, own, near = attention_forward_own(
        low_wide, high_wide, me, after(query, far_sum), nat, values, proj_t
    )
    kept = (normed1, query, keys, nat, values, proj_t, ctx_own, log_own, ctx_far, log_far)
    gain_one = proj_t[4 * lanes : 4 * lanes + 1].astype(F32)
    gain_two = proj_t[4 * lanes + 1 : 4 * lanes + 2].astype(F32)
    inputs = tokens.astype(F32)
    cots = (cotangent, swap(cotangent, "tp", 1))
    near, came = lax.optimization_barrier((near, swap(far_sum, "tp", 2)))
    h_mid = inputs + sum_rows(own, near, came)
    normal2, inverse2 = center_rows(h_mid)
    normed2 = (normal2 * gain_two).astype(BF16)
    full2 = (normed2, swap(normed2, "tp", 1))
    spot = me[1:]
    d_own, d_near, hidden, *early = mlp(
        ring, direct, spot, full2, cots, whole_rest, 2 * units
    )
    d_normed2 = pair_sum(d_own, d_near)
    d_mid = cotangent.astype(F32) + norm_pull(normal2, inverse2, gain_two, d_normed2)
    d_low = d_mid.astype(BF16)
    d_attn = gather_rows(d_low)

    out_own, out_near = down(after(hidden, d_attn[1]), whole_rest)
    output = (h_mid + pair_sum(out_own, out_near)).astype(BF16)
    if direct:
        came = lax.optimization_barrier((early[3:], d_attn[1]))[0]
        came = [swap(part, "fsdp", 2 * at) for at, part in enumerate(came, 1)]
        sent = swap(early[1], "fsdp", 1)
        sent, came, out_own = lax.optimization_barrier((sent, came, out_own))
        sums = (early[0].astype(F32) + sent.astype(F32)).astype(BF16)
        sums = [sums[at * slab : (at + 1) * slab] for at in range(ring // 2)]
        last_sums = sum([part.astype(F32) for part in came], early[2].astype(F32)).astype(BF16)
        d_attn, sums, last_sums, output = lax.optimization_barrier(
            (d_attn, sums, last_sums, output)
        )
        sums = [sums[0]] + [swap(sums[at], "fsdp", 2 * at) for at in range(1, ring // 2)]
        sums = sums + [last_sums[:slab], swap(last_sums[slab:], "fsdp", 1)]

    d_parts = attention_backward(
        ring, direct, low, high, me, d_attn, kept, cosine, sine
    )
    if direct:
        d_parts, sums = lax.optimization_barrier((d_parts, sums))
    late = d_parts[4:]
    far_sum = sum_far(*d_parts[2:4])
    d_normed1 = sum_rows(*d_parts[:2], swap(far_sum, "tp", 2))
    if direct:
        sums = lax.optimization_barrier((sums, far_sum))[0]
        sum_early = jnp.concatenate(
            [
                sum(part.astype(F32) for part in sums[: ring // 2]),
                sums[-2].astype(F32) + sums[-1].astype(F32),
            ],
            axis=1,
        )
        own_late = scatter_slabs(pair_slabs(after(late[0], far_sum), late[1]))
    else:
        sum_early = lax.psum_scatter(jnp.concatenate(early, axis=1), "fsdp", scatter_dimension=0, tiled=True)
        own_late = lax.psum_scatter(late[0], "fsdp", scatter_dimension=0, tiled=True).astype(F32)
    halves = [
        jnp.concatenate(
            [sum_early[:, (2 * k + side) * units : (2 * k + side + 1) * units] for k in range(3)],
            axis=1,
        )
        for side in range(2)
    ]
    own_early = halves[0].astype(F32) + swap(halves[1].astype(BF16), "tp", 2).astype(F32)
    normal1, inverse1 = center_rows(inputs)
    grad_tokens = (d_mid + norm_pull(normal1, inverse1, gain_one, d_normed1)).astype(BF16)

    sum_proj = own_late[:, : 3 * lanes]
    terms = jnp.stack(
        [
            jnp.sum(sum_proj * own_proj.astype(F32), axis=1),
            jnp.sum(own_early[:, : 2 * units] * mine[:, : 2 * units].astype(F32), axis=1),
        ]
    ) / gains.astype(F32)
    grad_gains = terms + swap(terms, "tp", 1) + swap(terms, "tp", 2) + swap(terms, "tp", 3)
    grad_qkv = jnp.transpose(sum_proj.reshape(slab, 3, lanes), (1, 0, 2))
    grad_in = jnp.stack([own_early[:, :units], own_early[:, units : 2 * units]])
    grad_out = own_late[:, 3 * lanes :].T
    grad_down = own_early[:, 2 * units :].T
    return (output, grad_tokens, grad_qkv, grad_out, grad_in, grad_down, grad_gains)


def solution(mesh):
    rows = P(("fsdp", "tp"), None)
    weights = (P(None, "fsdp", "tp"), P("tp", "fsdp"), P(None, "fsdp", "tp"), P("tp", "fsdp"))
    gains = P(None, "fsdp")
    return jax.shard_map(
        shards,
        mesh=mesh,
        in_specs=(rows, P("fsdp", None), *weights, gains, rows),
        out_specs=(rows, rows, *weights, gains),
        check_vma=False,
    )
```

```python
import functools

import jax
import jax.numpy as jnp
from jax import lax
from jax.experimental import pallas as pl
from jax.experimental.pallas import tpu as pltpu
from jax.sharding import PartitionSpec as P

HEAD_DIM = 64
HALF = HEAD_DIM // 2
WIDE = 128
TILE = 256
FAR = -1e30
VMEM_BYTES = 56 * 1024 * 1024
BF16 = jnp.bfloat16
F32 = jnp.float32

NN = (((1,), (0,)), ((), ()))
NT = (((1,), (1,)), ((), ()))
TN = (((0,), (0,)), ((), ()))


def mm(left, right, dims=NN):
    return lax.dot_general(left, right, dims, preferred_element_type=F32)


def positions(lengths, total):
    ends = jnp.cumsum(lengths)
    starts = ends - lengths
    index = jnp.arange(total, dtype=jnp.int32)
    segment = jnp.sum((index[:, None] >= ends[None, :]).astype(jnp.int32), axis=1)
    onehot = segment[:, None] == jnp.arange(lengths.shape[0], dtype=jnp.int32)[None, :]
    first = jnp.sum(jnp.where(onehot, starts[None, :], 0), axis=1)
    last = jnp.sum(jnp.where(onehot, ends[None, :], 0), axis=1)
    return (segment, index - first, first, last)


def rope_tables(place):
    freq = jnp.exp(
        -jnp.log(jnp.float32(160000.0)) * jnp.arange(HALF, dtype=F32) * (2.0 / HEAD_DIM)
    )
    angle = freq[:, None] * place.astype(F32)[None, :]
    return (jnp.cos(angle), jnp.sin(angle))


def pieces_of(row):
    high = row.astype(BF16).astype(F32)
    rest = row - high
    middle = rest.astype(BF16).astype(F32)
    return high, middle, rest - middle


def extend(body, rows):
    rest = WIDE - body.shape[0] - sum(row.shape[0] for row in rows)
    return jnp.concatenate([body, *rows, jnp.zeros((rest, body.shape[1]), F32)], axis=0)


def slot_of(at, me, split):
    return ((at // split) ^ me) * split + at % split


def tile(at):
    return pl.ds(pl.multiple_of(at * TILE, TILE), TILE)


def place_shards(spot, shards_in, flat_ref):
    slab = shards_in[0].shape[0]
    for index, shard in enumerate(shards_in):
        place = pl.multiple_of((spot ^ index) * slab, slab)
        flat_ref[pl.ds(place, slab), :] = shard[...]


def store_slabs(spot, ring, flat_ref, outs):
    if len(outs) == 1:
        outs[0][...] = flat_ref[...]
        return
    slab = flat_ref.shape[0] // ring
    for index in range(ring):
        place = pl.multiple_of((spot ^ index) * slab, slab)
        target = slice(index // 2 * slab, (index // 2 + 1) * slab)
        outs[index % 2][target, :] = flat_ref[pl.ds(place, slab), :]


def forward_kernel(blocks, low_ref, high_ref, me_ref, *refs):
    toks = refs[:4]
    seg_ref, cos_ref, sin_ref = refs[4:7]
    shards_in = refs[7 : 7 + blocks]
    normed_ref, query_ref, keys_ref, values_ref, ctx_ref, log_ref, wproj_ref = refs[
        7 + blocks : 14 + blocks
    ]
    attns = refs[14 + blocks : 18 + blocks]
    nat_ref, flat_ref, part_ref = refs[18 + blocks :]
    group = normed_ref.shape[0]
    heads = query_ref.shape[0]
    lanes = heads * HEAD_DIM
    parts = 8
    count = group // TILE
    split = count // 4
    wide = group // 4
    me = me_ref[0]

    place_shards(me_ref[1] if blocks > 1 else 0, shards_in, flat_ref)
    wproj_ref[...] = flat_ref[...].T
    gain = wproj_ref[4 * lanes : 4 * lanes + 16, :].astype(F32)[:1]

    for slot in range(count):
        rows = toks[slot // split][slot % split * TILE : (slot % split + 1) * TILE, :].astype(F32)
        center = rows - jnp.mean(rows, axis=-1, keepdims=True)
        spread = jnp.mean(center * center, axis=-1, keepdims=True)
        normed = (center * lax.rsqrt(spread + 1e-05) * gain).astype(BF16)
        normed_ref[slot * TILE : (slot + 1) * TILE, :] = normed

    def project(slot):
        return mm(wproj_ref[: 3 * lanes, :], normed_ref[slot * TILE : (slot + 1) * TILE, :], NT)

    upcoming = project(0)
    for slot in range(count):
        mixed = upcoming
        if slot + 1 < count:
            upcoming = project(slot + 1)
        here = slice(slot * TILE, (slot + 1) * TILE)
        there = tile(slot_of(slot, me, split))
        cosine = cos_ref[:, there]
        sine = sin_ref[:, there]
        segment = seg_ref[:, there]
        same = (segment == lax.broadcasted_iota(jnp.int32, (parts, TILE), 0)).astype(F32)
        ones = jnp.ones((2 * parts, TILE), F32)

        def rotated(top):
            first = mixed[top : top + HALF]
            second = mixed[top + HALF : top + HEAD_DIM]
            return jnp.concatenate(
                [first * cosine - second * sine, second * cosine + first * sine], axis=0
            )

        keys = []
        for head in range(heads):
            top = head * HEAD_DIM
            query = rotated(top) * (HEAD_DIM ** (-0.5))
            query_ref[head, :, here] = extend(query, [(1.0 - same) * FAR]).astype(BF16)
            keys.append(extend(rotated(lanes + top), [same, ones[:parts]]).astype(BF16))
            keys_ref[head, :, here] = keys[head][:HEAD_DIM]
            value = mixed[2 * lanes + top : 2 * lanes + top + HEAD_DIM]
            values_ref[head, :, here] = jnp.concatenate([value, ones], axis=0).astype(BF16)
        for head in range(heads):
            nat_ref[head, here, :] = keys[head].T

    every = range(heads)

    @pl.loop(0, 4)
    def attend(step):
        here = pl.ds(pl.multiple_of((step ^ me) * wide, wide), wide)

        def inner(at, carry):
            there = tile(slot_of(at, me, split))
            tops, accs = carry
            scores = [mm(nat_ref[h, there, :], query_ref[h, :, here]) for h in every]
            new = [jnp.maximum(tops[h], jnp.max(scores[h], axis=0, keepdims=True)) for h in every]
            expo = [jnp.exp(scores[h] - new[h]).astype(BF16) for h in every]
            scale = [jnp.exp(tops[h] - new[h]) for h in every]
            accs = [
                accs[h] * scale[h] + mm(values_ref[h, :, there], expo[h]) for h in every
            ]
            return new, accs

        start = (
            [jnp.full((1, wide), -jnp.inf, F32) for _ in every],
            [jnp.zeros((HEAD_DIM + 2 * parts, wide), F32) for _ in every],
        )
        tops, accs = lax.fori_loop(low_ref[step], high_ref[step], inner, start)
        totals = [acc[HEAD_DIM : HEAD_DIM + 1] for acc in accs]
        ctx = [acc[:HEAD_DIM] / total for acc, total in zip(accs, totals)]
        ctx = jnp.concatenate(ctx, axis=0).astype(BF16)
        ctx_ref[:, here] = ctx
        logs = [top + jnp.log(total) for top, total in zip(tops, totals)]
        log_ref[:, here] = jnp.concatenate(
            logs + [jnp.zeros((8 - heads, wide), F32)], axis=0
        )
        part_ref[here, :] = mm(ctx.T, wproj_ref[3 * lanes : 4 * lanes, :]).astype(BF16)

    for index in range(4):
        attns[index][...] = part_ref[index * wide : (index + 1) * wide, :]


def backward_kernel(ring, low_ref, high_ref, me_ref, *refs):
    dattn = refs[:4]
    (
        normed_ref, query_ref, keys_ref, values_ref, ctx_ref, log_ref, wproj_ref,
        seg_ref, cos_ref, sin_ref,
    ) = refs[4:14]
    dnormeds = refs[14:18]
    grads = refs[18:-9]
    qx_ref, kx_ref, vx_ref, dx_ref, dq_ref, dmix_ref, all_ref, tall_ref, flat_ref = refs[-9:]
    group = normed_ref.shape[0]
    lanes = ctx_ref.shape[0]
    heads = lanes // HEAD_DIM
    parts = 8
    count = group // TILE
    split = count // 4
    me = me_ref[0]
    scale = HEAD_DIM ** (-0.5)
    every = range(heads)

    def pull_context(slot):
        piece = dattn[slot // split][slot % split * TILE : (slot % split + 1) * TILE, :]
        all_ref[slot * TILE : (slot + 1) * TILE, :] = piece
        return mm(wproj_ref[3 * lanes : 4 * lanes, :], piece, NT)

    upcoming = pull_context(0)
    for slot in range(count):
        here = slice(slot * TILE, (slot + 1) * TILE)
        there = tile(slot_of(slot, me, split))
        d_ctx = upcoming.astype(BF16).astype(F32)
        if slot + 1 < count:
            upcoming = pull_context(slot + 1)
        ctx = ctx_ref[:, here].astype(F32)
        segment = seg_ref[:, there]
        same = (segment == lax.broadcasted_iota(jnp.int32, (parts, TILE), 0)).astype(F32)
        ones = jnp.ones((parts, TILE), F32)
        blank = jnp.zeros((parts - 3, TILE), F32)
        logs = log_ref[:, here]
        natural = []
        for head in every:
            rows = slice(head * HEAD_DIM, (head + 1) * HEAD_DIM)
            delta = -jnp.sum(d_ctx[rows] * ctx[rows], axis=0, keepdims=True)
            dx_ref[head, :, here] = extend(d_ctx[rows], [*pieces_of(delta), blank]).astype(BF16)
            log = -logs[head : head + 1]
            query = query_ref[head, : HEAD_DIM + parts, here].astype(F32)
            qx_ref[head, :, here] = extend(query, [*pieces_of(log), blank]).astype(BF16)
            key = keys_ref[head, :, here].astype(F32)
            value = values_ref[head, :HEAD_DIM, here].astype(F32)
            natural.append(
                (extend(key, [same, ones]).astype(BF16), extend(value, [ones]).astype(BF16))
            )
            dq_ref[head, :, here] = jnp.zeros((HEAD_DIM, TILE), F32)
        for head in every:
            kx_ref[head, here, :] = natural[head][0].T
            vx_ref[head, here, :] = natural[head][1].T

    def turned_back(grad, where):
        cosine = cos_ref[:, where]
        sine = sin_ref[:, where]
        first = grad[:HALF]
        second = grad[HALF:]
        return jnp.concatenate(
            [first * cosine + second * sine, second * cosine - first * sine], axis=0
        ).astype(BF16)

    @pl.loop(0, count)
    def attend(step):
        here = tile(slot_of(step, me, split))

        def inner(at, carry):
            there = tile(slot_of(at, me, split))
            d_keys, d_values = carry
            scores = [mm(kx_ref[h, here, :], qx_ref[h, :, there]) for h in every]
            d_probs = [mm(vx_ref[h, here, :], dx_ref[h, :, there]) for h in every]
            probs = [jnp.exp(score) for score in scores]
            d_scores = [(probs[h] * d_probs[h]).astype(BF16) for h in every]
            low_probs = [prob.astype(BF16) for prob in probs]
            d_values = [
                d_values[h] + mm(dx_ref[h, :HEAD_DIM, there], low_probs[h], NT) for h in every
            ]
            d_keys = [
                d_keys[h] + mm(qx_ref[h, :HEAD_DIM, there], d_scores[h], NT) for h in every
            ]
            for h in every:
                dq_ref[h, :, there] += mm(keys_ref[h, :, here], d_scores[h])
            return d_keys, d_values

        zero = [jnp.zeros((HEAD_DIM, TILE), F32) for _ in every]
        d_keys, d_values = lax.fori_loop(low_ref[step], high_ref[step], inner, (zero, zero))
        for head in every:
            top = head * HEAD_DIM
            turned = turned_back(d_keys[head], tile(step))
            dmix_ref[lanes + top : lanes + top + HEAD_DIM, here] = turned
            d_value = d_values[head].astype(BF16)
            dmix_ref[2 * lanes + top : 2 * lanes + top + HEAD_DIM, here] = d_value

    for slot in range(count):
        here = slice(slot * TILE, (slot + 1) * TILE)
        there = tile(slot_of(slot, me, split))
        for head in every:
            top = head * HEAD_DIM
            turned = turned_back(dq_ref[head, :, here] * scale, there)
            dmix_ref[top : top + HEAD_DIM, here] = turned

    for step in range(3):
        rows = slice(step * lanes, (step + 1) * lanes)
        tall_ref[rows, :] = mm(dmix_ref[rows, :], normed_ref[...]).astype(BF16)
    tall_ref[3 * lanes :, :] = mm(ctx_ref[...], all_ref[...]).astype(BF16)
    flat_ref[...] = tall_ref[...].T
    store_slabs(me_ref[1], ring, flat_ref, grads)

    for slot in range(count):
        here = slice(slot * TILE, (slot + 1) * TILE)
        d_normed = mm(dmix_ref[:, here].T, wproj_ref[: 3 * lanes, :])
        inside = slice(slot % split * TILE, (slot % split + 1) * TILE)
        dnormeds[slot // split][inside, :] = d_normed.astype(BF16)


def mlp_kernel(ring, me_ref, *refs):
    own_ref, near_ref, cot_ref, cot_near_ref, rest_ref = refs[:5]
    d_own_ref, d_near_ref, hidden_ref, d_both_ref = refs[5:9]
    grads = refs[9:-3]
    pair_ref, cots_ref, flat_ref = refs[-3:]
    rows, model = own_ref.shape
    wide = hidden_ref.shape[1]
    units = flat_ref.shape[1]
    count = 2 * rows // TILE
    half = count // 2

    def start(slot):
        inside = slice(slot % half * TILE, (slot % half + 1) * TILE)
        normed = (own_ref, near_ref)[slot // half][inside, :]
        cot = (cot_ref, cot_near_ref)[slot // half][inside, :]
        cots_ref[:, slot * TILE : (slot + 1) * TILE] = cot.T
        return mm(normed, rest_ref[:, : 2 * wide]), mm(cot, rest_ref[:, 2 * wide :])

    upcoming = start(0)
    pair_ref[...] = rest_ref[:, : 2 * wide].T
    for slot in range(count):
        both, d_hid = upcoming
        if slot + 1 < count:
            upcoming = start(slot + 1)
        here = slice(slot * TILE, (slot + 1) * TILE)
        inside = slice(slot % half * TILE, (slot % half + 1) * TILE)
        up_in = both[:, :wide]
        gate_in = both[:, wide:]
        share = 0.5 + 0.5 * lax.erf(up_in * (0.5**0.5))
        slope = share + up_in * jnp.exp(-0.5 * up_in * up_in) * 0.3989422804014327
        curve = up_in * share
        hidden_ref[here, :] = (curve * gate_in).astype(BF16)
        d_up = (d_hid * gate_in * slope).astype(BF16)
        d_gate = (d_hid * curve).astype(BF16)
        d_both_ref[here, :wide] = d_up
        d_both_ref[here, wide:] = d_gate
        d_normed = mm(d_up, pair_ref[:wide, :]) + mm(d_gate, pair_ref[wide:, :])
        (d_own_ref, d_near_ref)[slot // half][inside, :] = d_normed.astype(BF16)
    flat_ref[...] = mm(cots_ref[...], hidden_ref[...])[:, :units].astype(BF16)
    store_slabs(me_ref[0], ring, flat_ref, grads)


def mlp_late_kernel(ring, me_ref, *refs):
    own_ref, near_ref, d_both_ref = refs[:3]
    grads = refs[3:-2]
    rows_ref, flat_ref = refs[-2:]
    rows = own_ref.shape[0]
    wide = d_both_ref.shape[1] // 2
    units = flat_ref.shape[1] // 2
    rows_ref[:, :rows] = own_ref[...].T
    rows_ref[:, rows:] = near_ref[...].T
    grad = mm(rows_ref[...], d_both_ref[...]).astype(BF16)
    flat_ref[...] = jnp.concatenate([grad[:, :units], grad[:, wide : wide + units]], axis=1)
    store_slabs(me_ref[0], ring, flat_ref, grads)


def down_kernel(hidden_ref, rest_ref, own_ref, near_ref, last_ref):
    rows = own_ref.shape[0]
    last_ref[...] = rest_ref[:, 2 * hidden_ref.shape[1] :].T
    own_ref[...] = mm(hidden_ref[:rows, :], last_ref[...]).astype(BF16)
    near_ref[...] = mm(hidden_ref[rows:, :], last_ref[...]).astype(BF16)


def vmem_spec():
    return pl.BlockSpec(memory_space=pltpu.VMEM)


def smem_spec():
    return pl.BlockSpec(memory_space=pltpu.SMEM)


def attention_forward(low, high, me, toks, seg, cosine, sine, shards_in, lanes):
    rows, model = toks[0].shape
    group = 4 * rows
    heads = lanes // HEAD_DIM
    blocks = len(shards_in)
    width = shards_in[0].shape[1]
    shape = jax.ShapeDtypeStruct
    return pl.pallas_call(
        functools.partial(forward_kernel, blocks),
        out_shape=(
            shape((group, model), BF16),
            shape((heads, WIDE, group), BF16),
            shape((heads, HEAD_DIM, group), BF16),
            shape((heads, HEAD_DIM + 16, group), BF16),
            shape((lanes, group), BF16),
            shape((8, group), F32),
            shape((width, model), BF16),
            *[shape((rows, model), BF16) for _ in range(4)],
        ),
        in_specs=[smem_spec()] * 3 + [vmem_spec()] * (7 + blocks),
        out_specs=[vmem_spec()] * 11,
        scratch_shapes=[
            pltpu.VMEM((heads, group, WIDE), BF16),
            pltpu.VMEM((model, width), BF16),
            pltpu.VMEM((group, model), BF16),
        ],
        compiler_params=pltpu.CompilerParams(vmem_limit_bytes=VMEM_BYTES),
        cost_estimate=pl.CostEstimate(
            flops=2 * group * model * lanes * 4 + 2 * group * group * lanes,
            bytes_accessed=group * model * 8,
            transcendentals=group * group,
        ),
        name="attention_forward",
    )(low, high, me, *toks, seg, cosine, sine, *shards_in)


def attention_backward(ring, direct, low, high, me, d_attn, kept, seg, cosine, sine):
    rows, model = d_attn[0].shape
    group = 4 * rows
    lanes = kept[4].shape[0]
    heads = lanes // HEAD_DIM
    shape = jax.ShapeDtypeStruct
    outs = 2 if direct else 1
    return pl.pallas_call(
        functools.partial(backward_kernel, ring),
        out_shape=(
            *[shape((rows, model), BF16) for _ in range(4)],
            *[shape((model // outs, 4 * lanes), BF16) for _ in range(outs)],
        ),
        in_specs=[smem_spec()] * 3 + [vmem_spec()] * 14,
        out_specs=[vmem_spec()] * (4 + outs),
        scratch_shapes=[
            pltpu.VMEM((heads, WIDE, group), BF16),
            pltpu.VMEM((heads, group, WIDE), BF16),
            pltpu.VMEM((heads, group, WIDE), BF16),
            pltpu.VMEM((heads, WIDE, group), BF16),
            pltpu.VMEM((heads, HEAD_DIM, group), F32),
            pltpu.VMEM((3 * lanes, group), BF16),
            pltpu.VMEM((group, model), BF16),
            pltpu.VMEM((4 * lanes, model), BF16),
            pltpu.VMEM((model, 4 * lanes), BF16),
        ],
        compiler_params=pltpu.CompilerParams(vmem_limit_bytes=VMEM_BYTES),
        cost_estimate=pl.CostEstimate(
            flops=2 * group * model * lanes * 64,
            bytes_accessed=group * model * 12,
            transcendentals=group * group,
        ),
        name="attention_backward",
    )(low, high, me, *d_attn, *kept, seg, cosine, sine)


def mlp(ring, direct, spot, rows_in, cots, rest, units):
    rows, model = rows_in[0].shape
    wide = rest.shape[1] // 3
    outs = 2 if direct else 1
    shape = jax.ShapeDtypeStruct
    return pl.pallas_call(
        functools.partial(mlp_kernel, ring),
        out_shape=(
            shape((rows, model), BF16),
            shape((rows, model), BF16),
            shape((2 * rows, wide), BF16),
            shape((2 * rows, 2 * wide), BF16),
            *[shape((model // outs, units), BF16) for _ in range(outs)],
        ),
        in_specs=[smem_spec()] + [vmem_spec()] * 5,
        out_specs=[vmem_spec()] * (4 + outs),
        scratch_shapes=[
            pltpu.VMEM((2 * wide, model), BF16),
            pltpu.VMEM((model, 2 * rows), BF16),
            pltpu.VMEM((model, units), BF16),
        ],
        compiler_params=pltpu.CompilerParams(vmem_limit_bytes=VMEM_BYTES),
        cost_estimate=pl.CostEstimate(
            flops=24 * rows * model * wide, bytes_accessed=rows * model * 16, transcendentals=0
        ),
        name="mlp",
    )(spot, *rows_in, *cots, rest)


def mlp_late(ring, direct, spot, rows_in, d_both, units):
    rows, model = rows_in[0].shape
    wide = d_both.shape[1] // 2
    outs = 2 if direct else 1
    shape = jax.ShapeDtypeStruct
    return pl.pallas_call(
        functools.partial(mlp_late_kernel, ring),
        out_shape=tuple(shape((model // outs, 2 * units), BF16) for _ in range(outs)),
        in_specs=[smem_spec()] + [vmem_spec()] * 3,
        out_specs=(vmem_spec(),) * outs,
        scratch_shapes=[
            pltpu.VMEM((model, 2 * rows), BF16),
            pltpu.VMEM((model, 2 * units), BF16),
        ],
        compiler_params=pltpu.CompilerParams(vmem_limit_bytes=VMEM_BYTES),
        cost_estimate=pl.CostEstimate(
            flops=8 * rows * model * wide, bytes_accessed=rows * model * 12, transcendentals=0
        ),
        name="mlp_late",
    )(spot, *rows_in, d_both)


def down(hidden, rest):
    rows, wide = hidden.shape
    model = rest.shape[0]
    out = jax.ShapeDtypeStruct((rows // 2, model), BF16)
    return pl.pallas_call(
        down_kernel,
        out_shape=(out, out),
        in_specs=[vmem_spec()] * 2,
        out_specs=[vmem_spec()] * 2,
        scratch_shapes=[pltpu.VMEM((wide, model), BF16)],
        compiler_params=pltpu.CompilerParams(vmem_limit_bytes=VMEM_BYTES),
        cost_estimate=pl.CostEstimate(
            flops=2 * rows * model * wide, bytes_accessed=rows * model * 6, transcendentals=0
        ),
        name="down",
    )(hidden, rest)


def swap(value, axis, bit):
    size = lax.axis_size(axis)
    return lax.ppermute(value, axis, [(i, i ^ bit) for i in range(size)])


def gather_rows(rows):
    far = swap(rows, "tp", 2)
    return (rows, swap(rows, "tp", 1), far, swap(far, "tp", 1))


def scatter_rows(own, near, far, corner):
    far_sum = (far.astype(F32) + swap(corner, "tp", 1).astype(F32)).astype(BF16)
    came = swap(far_sum, "tp", 2)
    mine = own.astype(F32) + swap(near, "tp", 1).astype(F32)
    return mine + came.astype(F32), far_sum


def pair_sum(own, near):
    return own.astype(F32) + swap(near, "tp", 1).astype(F32)


def swaps_over(axis):
    size = lax.axis_size(axis)
    return size in (2, 4, 8)


def gather_slabs(slab):
    evens = [slab] + [swap(slab, "fsdp", bit) for bit in range(2, lax.axis_size("fsdp"), 2)]
    return [block for even in evens for block in (even, swap(even, "fsdp", 1))]


def pair_slabs(keep, send):
    return (keep.astype(F32) + swap(send, "fsdp", 1).astype(F32)).astype(BF16)


def scatter_slabs(sums):
    ring = lax.axis_size("fsdp")
    slab = 2 * sums.shape[0] // ring
    own = sums[:slab].astype(F32)
    for at in range(1, ring // 2):
        own = own + swap(sums[at * slab : (at + 1) * slab], "fsdp", 2 * at).astype(F32)
    return own


def after(value, *others):
    return lax.optimization_barrier((value, *others))[0]


def center_rows(values):
    center = values - jnp.mean(values, axis=-1, keepdims=True)
    spread = jnp.mean(center * center, axis=-1, keepdims=True)
    inverse = lax.rsqrt(spread + 1e-05)
    return center * inverse, inverse


def norm_pull(normal, inverse, gain, grad):
    scaled = grad * gain
    mean = jnp.mean(scaled, axis=-1, keepdims=True)
    along = jnp.mean(scaled * normal, axis=-1, keepdims=True)
    return (scaled - mean - normal * along) * inverse


def shards(tokens, seq_lengths, w_qkv, w_out, w_in, w_down, gains, cotangent):
    rows, model = tokens.shape
    slab = w_qkv.shape[1]
    lanes = w_qkv.shape[2]
    units = w_in.shape[2]
    group = rows * lax.axis_size("tp")
    ring = lax.axis_size("fsdp")
    direct = swaps_over("fsdp")
    at_fsdp = lax.axis_index("fsdp")

    own_proj = jnp.transpose(w_qkv, (1, 0, 2)).reshape(slab, 3 * lanes)
    spare = -(4 * lanes + gains.shape[0]) % WIDE
    first = jnp.concatenate(
        [own_proj, w_out.T, gains.T, jnp.zeros((slab, spare), BF16)], axis=1
    )
    far = swap(tokens, "tp", 2)
    near = swap(tokens, "tp", 1)
    if direct:
        first_parts = gather_slabs(after(first, near))
    else:
        first_parts = [lax.all_gather(first, "fsdp", axis=0, tiled=True)]
    corner = swap(after(far, *first_parts), "tp", 1)
    toks = (tokens, near, far, corner)
    mine = jnp.concatenate([w_in[0], w_in[1], w_down.T], axis=1)
    other = swap(after(mine, far), "tp", 2)
    spare = jnp.zeros((slab, -2 * units % WIDE), BF16)
    rest = jnp.concatenate(
        [
            part
            for k in range(3)
            for part in (mine[:, k * units : (k + 1) * units], other[:, k * units : (k + 1) * units], spare)
        ],
        axis=1,
    )
    rest = after(rest, *first_parts)
    whole_rest = lax.all_gather(rest, "fsdp", axis=0, tiled=True)

    segment, place, seq_first, seq_last = positions(seq_lengths[0], group)
    cosine, sine = rope_tables(place)
    low = seq_first[::TILE] // TILE
    high = (seq_last[TILE - 1 :: TILE] + TILE - 1) // TILE
    low_wide = seq_first[::rows] // TILE
    high_wide = (seq_last[rows - 1 :: rows] + TILE - 1) // TILE
    seg = segment[None, :]
    me = jnp.stack([lax.axis_index("tp"), at_fsdp]).astype(jnp.int32)

    *kept, proj_t, own, near, far, corner = attention_forward(
        low_wide, high_wide, me, toks, seg, cosine, sine, first_parts, lanes
    )
    gain_one = proj_t[4 * lanes : 4 * lanes + 1].astype(F32)
    gain_two = proj_t[4 * lanes + 1 : 4 * lanes + 2].astype(F32)
    inputs = tokens.astype(F32)
    cots = (cotangent, swap(cotangent, "tp", 1))
    h_mid = inputs + scatter_rows(own, near, far, corner)[0]
    normal2, inverse2 = center_rows(h_mid)
    normed2 = (normal2 * gain_two).astype(BF16)
    full2 = (normed2, swap(normed2, "tp", 1))
    spot = me[1:]
    d_own, d_near, hidden, d_both, *last_halves = mlp(
        ring, direct, spot, full2, cots, whole_rest, 2 * units
    )
    d_normed2 = pair_sum(d_own, d_near)
    d_mid = cotangent.astype(F32) + norm_pull(normal2, inverse2, gain_two, d_normed2)
    d_low = d_mid.astype(BF16)
    d_attn = gather_rows(d_low)

    pair_halves = mlp_late(
        ring, direct, spot, full2, after(d_both, d_attn[1]), 2 * units
    )
    out_own, out_near = down(after(hidden, pair_halves[0]), whole_rest)
    output = (h_mid + pair_sum(out_own, out_near)).astype(BF16)
    if direct:
        pair_sums = pair_slabs(after(pair_halves[0], out_near), pair_halves[1]).reshape(ring // 2, slab, 4 * units)
        last_sums = pair_slabs(*last_halves).reshape(ring // 2, slab, 2 * units)
        sums = [
            jnp.concatenate([pair_sums[at], last_sums[at]], axis=1) for at in range(ring // 2)
        ]
        d_attn, sums, output = lax.optimization_barrier((d_attn, sums, output))
        sums = [sums[0]] + [swap(sums[at], "fsdp", 2 * at) for at in range(1, ring // 2)]

    d_parts = attention_backward(
        ring, direct, low, high, me, d_attn, (*kept, proj_t), seg, cosine, sine
    )
    if direct:
        d_parts, sums = lax.optimization_barrier((d_parts, sums))
    late = d_parts[4:]
    d_normed1, far_sum = scatter_rows(*d_parts[:4])
    if direct:
        sum_early = after(sums[0], far_sum).astype(F32)
        for at in range(1, ring // 2):
            sum_early = sum_early + sums[at].astype(F32)
        own_late = scatter_slabs(pair_slabs(after(late[0], far_sum), late[1]))
    else:
        early = jnp.concatenate([pair_halves[0], last_halves[0]], axis=1)
        sum_early = lax.psum_scatter(early, "fsdp", scatter_dimension=0, tiled=True)
        own_late = lax.psum_scatter(late[0], "fsdp", scatter_dimension=0, tiled=True).astype(F32)
    halves = [
        jnp.concatenate(
            [sum_early[:, (2 * k + side) * units : (2 * k + side + 1) * units] for k in range(3)],
            axis=1,
        )
        for side in range(2)
    ]
    own_early = halves[0].astype(F32) + swap(halves[1].astype(BF16), "tp", 2).astype(F32)
    normal1, inverse1 = center_rows(inputs)
    grad_tokens = (d_mid + norm_pull(normal1, inverse1, gain_one, d_normed1)).astype(BF16)

    sum_proj = own_late[:, : 3 * lanes]
    terms = jnp.stack(
        [
            jnp.sum(sum_proj * own_proj.astype(F32), axis=1),
            jnp.sum(own_early[:, : 2 * units] * mine[:, : 2 * units].astype(F32), axis=1),
        ]
    ) / gains.astype(F32)
    grad_gains = terms + swap(terms, "tp", 1) + swap(terms, "tp", 2) + swap(terms, "tp", 3)
    grad_qkv = jnp.transpose(sum_proj.reshape(slab, 3, lanes), (1, 0, 2))
    grad_in = jnp.stack([own_early[:, :units], own_early[:, units : 2 * units]])
    grad_out = own_late[:, 3 * lanes :].T
    grad_down = own_early[:, 2 * units :].T
    return (output, grad_tokens, grad_qkv, grad_out, grad_in, grad_down, grad_gains)


def solution(mesh):
    rows = P(("fsdp", "tp"), None)
    weights = (P(None, "fsdp", "tp"), P("tp", "fsdp"), P(None, "fsdp", "tp"), P("tp", "fsdp"))
    gains = P(None, "fsdp")
    return jax.shard_map(
        shards,
        mesh=mesh,
        in_specs=(rows, P("fsdp", None), *weights, gains, rows),
        out_specs=(rows, rows, *weights, gains),
        check_vma=False,
    )
```
